512 devices in a mesh: tm: 128 (over y, z, x_lo), batch: 4 (over x_hi, core).
Axes of the slice: x: 4 (x_hi: 2, x_lo: 2; x = x_hi * 2 + x_lo), y: 8, z: 8, core: 2. Of those that a mesh axis runs over, the one named last changes fastest.
Arguments:
- signal: bfloat16 [16, 16384, 64], P('batch', 'tm'), may hold values from -6 to 6
- skip_grad: bfloat16 [16, 16384, 128], P('batch', 'tm'), may hold values from -24 to 24
- stream_grad: bfloat16 [16, 16384, 64], P('batch', 'tm'), may hold values from -24 to 24
- w_past: bfloat16 [5, 64, 512], replicated, may hold values from -0.5 to 0.5
- w_now: bfloat16 [5, 64, 512], replicated, may hold values from -0.5 to 0.5
- w_res: bfloat16 [5, 256, 64], replicated, may hold values from -0.375 to 0.375
- w_skip: bfloat16 [5, 256, 128], replicated, may hold values from -0.375 to 0.375
Outputs:
- skip_out: bfloat16 [16, 16384, 128], P('batch', 'tm')
- stream_out: bfloat16 [16, 16384, 64], P('batch', 'tm')
- signal_cot: bfloat16 [16, 16384, 64], P('batch', 'tm')
- g_past: bfloat16 [5, 64, 512], replicated
- g_now: bfloat16 [5, 64, 512], replicated
- g_res: bfloat16 [5, 256, 64], replicated
- g_skip: bfloat16 [5, 256, 128], replicated
The draws below stay inside these ranges and needn't reach their ends.
All inputs are finite; a program needn't handle non-finite values.
Results may differ from the reference program's by a relative error of at most 0.015.
Values may be sent and summed in bfloat16 or wider, within the bound.
A program may use at most 64 MiB of HBM per device.

```python
import math
import jax
import jax.numpy as jnp
from jax import lax

RES = 64
GATE = 256
SKIP = 128
LAYERS = 5
BASE = 8
LEN = 16384
SEQS = 16


def rising_cotangent(key, width):
    time_ramp = 1.0 + 2.0 * jnp.arange(LEN, dtype=jnp.float32) / (LEN - 1)
    values_drawn = jax.random.truncated_normal(jax.random.fold_in(key, 7), -4.0, 4.0, (SEQS, LEN, width), jnp.float32)
    return (values_drawn * time_ramp[None, :, None]).astype(jnp.bfloat16)


def draw_skip_grad(key, part):
    return rising_cotangent(jax.random.fold_in(key, 11), SKIP)


def draw_stream_grad(key, part):
    return rising_cotangent(jax.random.fold_in(key, 13), RES)


def levels(rng, dims, split, least, high):
    gain = 1.0
    for dim, parts in split:
        heights = jax.random.uniform(jax.random.fold_in(jax.random.fold_in(rng, 6), dim), (parts,), jnp.float32, least / len(split), high / len(split))
        gain = gain * jnp.repeat(jnp.exp(heights), dims[dim] // parts).reshape((-1,) + (1,) * (len(dims) - 1 - dim))
    return gain


def normal_values(rng, extent, spread, limit, pieces=(), held_as=jnp.bfloat16):
    array = spread * jax.random.normal(rng, extent, jnp.float32)
    if pieces:
        array = array * levels(rng, extent, pieces, -0.22, 0.18)
    return jnp.clip(array, -limit, limit).astype(held_as)


def setup_inputs(seed: int = 0) -> dict:
    splits = jax.random.split(jax.random.key(seed), 8)
    signal = normal_values(splits[0], (SEQS, LEN, RES), 1.0, 6.0, ((0, 4), (1, 128)))
    skip_grad = draw_skip_grad(jax.random.fold_in(splits[7], 71), 0)
    stream_grad = draw_stream_grad(jax.random.fold_in(splits[7], 71), 0)
    w_past = normal_values(splits[3], (LAYERS, RES, 2 * GATE), (2 * RES) ** -0.5, 0.5)
    w_now = normal_values(splits[4], (LAYERS, RES, 2 * GATE), (2 * RES) ** -0.5, 0.5)
    w_res = normal_values(splits[5], (LAYERS, GATE, RES), GATE ** -0.5, 0.375)
    w_skip = normal_values(splits[6], (LAYERS, GATE, SKIP), GATE ** -0.5, 0.375)
    return dict(signal=signal, skip_grad=skip_grad, stream_grad=stream_grad, w_past=w_past, w_now=w_now, w_res=w_res, w_skip=w_skip)


def delay_rows(values, dilation):
    count = values.shape[0]
    lead = min(dilation, count)
    return jnp.concatenate([jnp.zeros((lead, values.shape[1]), values.dtype), values[:count - lead]], 0)

def advance_rows(values, dilation):
    count = values.shape[0]
    lead = min(dilation, count)
    return jnp.concatenate([values[lead:], jnp.zeros((lead, values.shape[1]), values.dtype)], 0)

def product(left, right):
    return jnp.dot(left, right, preferred_element_type=jnp.float32)

def reference(signal, skip_grad, stream_grad, w_past, w_now, w_res, w_skip):

    def one_sequence(items):
        stream, skip_cot, out_cot = items
        records = []
        skip_acc = jnp.zeros((stream.shape[0], SKIP), jnp.float32)
        for layer in range(LAYERS):
            dilation = BASE * 2 ** layer
            delayed = delay_rows(stream, dilation)
            preact = product(delayed, w_past[layer]) + product(stream, w_now[layer])
            gated = (jnp.tanh(preact[:, :GATE]) * jax.nn.sigmoid(preact[:, GATE:])).astype(jnp.bfloat16)
            records.append((delayed, stream, preact, gated))
            skip_acc = skip_acc + product(gated, w_skip[layer])
            stream = (stream.astype(jnp.float32) + product(gated, w_res[layer])).astype(jnp.bfloat16)
        flow = out_cot.astype(jnp.float32)
        grads = [None] * LAYERS
        for layer in reversed(range(LAYERS)):
            dilation = BASE * 2 ** layer
            delayed, current, preact, gated = records[layer]
            filt = jnp.tanh(preact[:, :GATE])
            sigm = jax.nn.sigmoid(preact[:, GATE:])
            flow_half = flow.astype(jnp.bfloat16)
            gated_cot = product(skip_cot, w_skip[layer].T) + product(flow_half, w_res[layer].T)
            pre_cot = jnp.concatenate([gated_cot * sigm * (1.0 - filt * filt), gated_cot * filt * sigm * (1.0 - sigm)], 1).astype(jnp.bfloat16)
            grads[layer] = (product(delayed.T, pre_cot), product(current.T, pre_cot), product(gated.T, flow_half), product(gated.T, skip_cot))
            past_cot = product(pre_cot, w_past[layer].T).astype(jnp.bfloat16)
            flow = flow + product(pre_cot, w_now[layer].T) + advance_rows(past_cot, dilation).astype(jnp.float32)
        stacked = tuple((jnp.stack([grads[layer][which] for layer in range(LAYERS)]) for which in range(4)))
        return (skip_acc.astype(jnp.bfloat16), stream, flow.astype(jnp.bfloat16), stacked)
    skip_out, stream_out, signal_cot, stacked = lax.map(one_sequence, (signal, skip_grad, stream_grad))
    scale = 1.0 / math.sqrt(SEQS * LEN)
    finals = tuple(((lax.optimization_barrier(jnp.sum(part_sum, axis=0)) * scale).astype(jnp.bfloat16) for part_sum in stacked))
    return (skip_out, stream_out, signal_cot, finals[0], finals[1], finals[2], finals[3])
```

```python
import functools
import math

import jax
import jax.numpy as jnp
from jax import lax
from jax.experimental import pallas as pl
from jax.experimental.pallas import tpu as pltpu
from jax.sharding import PartitionSpec as P

MESH = pl.DeviceIdType.MESH
F32 = jnp.float32
BF16 = jnp.bfloat16

RES = 64
GATE = 256
SKIP = 128
LAYERS = 5
SEQ = 4
ROWS = 128
N = SEQ * ROWS
DIL = (8, 16, 32, 64, 128)
LOW = (16, 32, 64, 128, 128)
CHUNK = 32
GROUP = 8
TILES = 8
WIRE = 7


def nn(left, right):
    return jnp.dot(left, right, preferred_element_type=F32)


def nt(left, right):
    return lax.dot_general(left, right, (((1,), (1,)), ((), ())), preferred_element_type=F32)


def tn(left, right):
    return lax.dot_general(left, right, (((0,), (0,)), ((), ())), preferred_element_type=F32)


def kernel(
    ny, nz, scale,
    signal, skip_grad, stream_grad, w_past, w_now, w_res, w_skip,
    skip_out, stream_out, signal_cot, g_past, g_now, g_res, g_skip,
    wx, wb, wf, wg, h2, xs, pre, gat_ext, gated, dfilt, dgate, skip_acc, flow, gcot, ycat, pcot,
    sig_in, h4_out, h4_in, past_out, past_in,
    grad, rs_in, part, part_in, line_in, final,
    halo_send, halo_recv, red_send, red_recv,
):
    tm = lax.axis_index("tm")
    batch = lax.axis_index("batch")
    blocks = ny * nz * 2
    x_lo = tm % 2
    zi = (tm // 2) % nz
    yi = tm // (2 * nz)
    ei = batch * 2 + x_lo
    tz = TILES // nz

    after = {"tm": (tm + 1) % blocks, "batch": batch}
    before = {"tm": (tm + blocks - 1) % blocks, "batch": batch}

    def group_peer(r):
        e = (ei + r) % GROUP
        return e, {"tm": tm - x_lo + e % 2, "batch": e // 2}

    def z_peer(r):
        z = (zi + r) % nz
        return z, {"tm": (yi * nz + z) * 2 + x_lo, "batch": batch}

    def y_peer(r):
        y = (yi + r) % ny
        return y, {"tm": (y * nz + zi) * 2 + x_lo, "batch": batch}

    partners = [after, before]
    partners += [group_peer(r)[1] for r in range(1, GROUP)]
    partners += [z_peer(r)[1] for r in range(1, nz)]
    partners += [y_peer(r)[1] for r in range(1, ny)]
    barrier = pltpu.get_barrier_semaphore()
    for partner in partners:
        pl.semaphore_signal(barrier, inc=1, device_id=partner, device_id_type=MESH)

    twice = (
        lax.broadcasted_iota(jnp.int32, (RES, 128), 1) % RES
        == lax.broadcasted_iota(jnp.int32, (RES, 128), 0)
    ).astype(F32).astype(BF16)
    low_half = lax.broadcasted_iota(jnp.int32, (1, 128), 1) < RES
    for j in range(LAYERS):
        wx[j, 0:64, :] = w_past[j]
        wx[j, 64:128, :] = w_now[j]
        wb[j, 0:64, :] = w_past[j]
        wb[j, 64:128, :] = w_past[j]
        wb[j, 128:192, :] = w_now[j]
        wb[j, 192:256, :] = w_now[j]
        wf[j, :, 0:128] = w_skip[j]
        wg[j, :, 0:128] = w_skip[j]
        both = nn(w_res[j], twice)
        wf[j, :, 128:256] = both.astype(BF16)
        wg[j, :, 128:256] = jnp.where(low_half, both, 0.0).astype(BF16)
    h2[0, :, 128:256, :] = nn(signal[...].reshape(N, RES), twice).reshape(SEQ, ROWS, 128)
    ycat[:, 0:128] = skip_grad[...].reshape(N, SKIP)
    flow[...] = nn(stream_grad[...].reshape(N, RES), twice)

    pl.semaphore_wait(barrier, len(partners))

    def halo_copy(which, src, dst, target):
        return pltpu.make_async_remote_copy(
            src_ref=src, dst_ref=dst, send_sem=halo_send.at[which], recv_sem=halo_recv.at[which],
            device_id=target, device_id_type=MESH,
        )

    first = halo_copy(5, signal, sig_in, after)
    first.start()
    has_before = jnp.where(tm > 0, 1.0, 0.0).astype(F32)
    has_after = jnp.where(tm < blocks - 1, 1.0, 0.0).astype(F32)
    skip_acc[...] = jnp.zeros_like(skip_acc)
    first.wait()
    h2[0, :, 0:128, :] = has_before * nn(sig_in[...].reshape(N, RES), twice).reshape(SEQ, ROWS, 128)

    def forward_rows(j, lo, hi):
        own = lo == 128
        span = hi - lo
        count = SEQ * span
        d = DIL[j]
        x = jnp.where(low_half, h2[j, :, lo - d : hi - d, :], h2[j, :, lo:hi, :])
        x = x.reshape(count, 128).astype(BF16)
        if own:
            xs[j] = x
        pre[0:count, :] = nn(x, wx[j])

        def step(i, carry):
            rows = pl.ds(pl.multiple_of(i * CHUNK, CHUNK), CHUNK)
            t = jnp.tanh(pre[rows, 0:GATE])
            s = 0.5 * jnp.tanh(0.5 * pre[rows, GATE : 2 * GATE]) + 0.5
            ts = t * s
            if own:
                gated[j, rows, :] = ts.astype(BF16)
                dfilt[j, rows, :] = s * (1.0 - t * t)
                dgate[j, rows, :] = ts * (1.0 - s)
            else:
                gat_ext[rows, :] = ts.astype(BF16)
            return carry

        lax.fori_loop(0, count // CHUNK, step, 0)
        g = gated[j] if own else gat_ext[0:count, :]
        y = nn(g, wf[j])
        if own:
            skip_acc[...] += y[:, 0:128]
        new = h2[j, :, lo:hi, :].reshape(count, 128) + y[:, 128:256]
        new = new.astype(BF16)
        if j + 1 < LAYERS:
            h2[j + 1, :, lo:hi, :] = new.astype(F32).reshape(SEQ, span, 128)
        return new

    for j in range(4):
        if LOW[j] < 128:
            forward_rows(j, LOW[j], 128)
        new = forward_rows(j, 128, 256)
    h4_out[...] = new.reshape(SEQ, ROWS, 128)
    second = halo_copy(6, h4_out, h4_in, after)
    second.start()
    second.wait()
    h2[4, :, 0:128, :] = has_before * h4_in[...].astype(F32)
    new = forward_rows(4, 128, 256)
    stream_out[...] = new[:, 0:RES].reshape(SEQ, ROWS, RES)
    skip_out[...] = skip_acc[...].astype(BF16).reshape(SEQ, ROWS, SKIP)

    def red_copy(stage, j, src, dst, target):
        pltpu.make_async_remote_copy(
            src_ref=src, dst_ref=dst, send_sem=red_send.at[stage, j], recv_sem=red_recv.at[stage, j],
            device_id=target, device_id_type=MESH,
        ).start()

    def red_wait(sem, ref):
        pltpu.make_async_copy(ref, ref, sem).wait()

    def exchange_a(j):
        for r in range(1, GROUP):
            e, peer = group_peer(r)
            red_copy(0, j, grad.at[j, e], rs_in.at[j, r - 1], peer)

    def exchange_b(j):
        red_wait(red_recv.at[0, j], rs_in.at[j])
        total = grad[j, ei].astype(F32)
        for r in range(GROUP - 1):
            total += rs_in[j, r].astype(F32)
        for k in range(WIRE):
            part[j, k // tz, k % tz] = total[:, 128 * k : 128 * k + 128].astype(BF16)
        for k in range(WIRE, TILES):
            part[j, k // tz, k % tz] = jnp.zeros((16, 128), BF16)
        for r in range(1, nz):
            z, peer = z_peer(r)
            red_copy(1, j, part.at[j, z], part_in.at[j, r - 1], peer)

    def exchange_c(j):
        if nz > 1:
            red_wait(red_recv.at[1, j], part_in.at[j])
        total = part[j, zi].astype(F32)
        for r in range(nz - 1):
            total += part_in[j, r].astype(F32)
        line_in[j, yi] = total.astype(BF16)
        for r in range(1, ny):
            _, peer = y_peer(r)
            red_copy(2, j, line_in.at[j, yi], line_in.at[j, yi], peer)

    def exchange_d(j):
        if ny > 1:
            red_wait(red_recv.at[2, j], line_in.at[j, pl.ds(0, ny - 1)])
        total = line_in[j, 0].astype(F32)
        for r in range(1, ny):
            total += line_in[j, r].astype(F32)
        final[j, ei, zi] = (total * scale).astype(BF16)
        for r in range(1, nz):
            _, peer = z_peer(r)
            red_copy(3, j, final.at[j, ei, zi], final.at[j, ei, zi], peer)

    def exchange_e(j):
        if nz > 1:
            red_wait(red_recv.at[3, j], final.at[j, 0, pl.ds(0, nz - 1)])
        for r in range(1, GROUP):
            _, peer = group_peer(r)
            red_copy(4, j, final.at[j, ei], final.at[j, ei], peer)

    def finish(j):
        red_wait(red_recv.at[4, j], final.at[j, pl.ds(0, GROUP - 1)])
        tile = [final[j, :, k // tz, k % tz].reshape(128, 128) for k in range(WIRE)]
        for k in range(4):
            g_past[j, :, 128 * k : 128 * k + 128] = tile[k][0:64]
            g_now[j, :, 128 * k : 128 * k + 128] = tile[k][64:128]
        g_res[j, 0:128, :] = tile[4][:, 0:RES]
        g_res[j, 128:256, :] = pltpu.roll(tile[4].astype(F32), RES, 1)[:, 0:RES].astype(BF16)
        g_skip[j, 0:128, :] = tile[5]
        g_skip[j, 128:256, :] = tile[6]

    stages = (exchange_a, exchange_b, exchange_c, exchange_d, exchange_e, finish)

    for j in reversed(range(LAYERS)):
        d = DIL[j]
        head = max(d, 16)
        ycat[:, 128:256] = flow[...].astype(BF16)
        gcot[...] = nt(ycat[...], wg[j])

        def step(i, carry, j=j):
            rows = pl.ds(pl.multiple_of(i * CHUNK, CHUNK), CHUNK)
            gc = gcot[rows, :]
            pcot[rows, 0:GATE] = (gc * dfilt[j, rows, :]).astype(BF16)
            pcot[rows, GATE : 2 * GATE] = (gc * dgate[j, rows, :]).astype(BF16)
            return carry

        lax.fori_loop(0, N // CHUNK, step, 0)
        back = nt(pcot[...], wb[j])
        past = back[:, 0:128].astype(BF16).reshape(SEQ, ROWS, 128)
        past_out[j, :, 0:head, :] = past[:, 0:head, :]
        third = halo_copy(
            j, past_out.at[j, :, pl.ds(0, head), :], past_in.at[j, :, pl.ds(0, head), :], before
        )
        third.start()
        flow[...] += back[:, 128:256]

        gx = tn(xs[j], pcot[...])
        gy = tn(gated[j], ycat[...])
        grad[j, :, :, 0:512] = gx.astype(BF16).reshape(GROUP, 16, 512)
        packed = jnp.where(low_half, gy[0:128, 128:256], gy[128:256, 128:256])
        grad[j, :, :, 512:640] = packed.astype(BF16).reshape(GROUP, 16, 128)
        grad[j, :, :, 640:768] = gy[0:128, 0:128].astype(BF16).reshape(GROUP, 16, 128)
        grad[j, :, :, 768:896] = gy[128:256, 0:128].astype(BF16).reshape(GROUP, 16, 128)

        for k in range(LAYERS - j):
            stages[k](j + k)

        third.wait()
        edge = has_after * past_in[j, :, 0:head, :].astype(F32)
        moved = edge[:, 0:d, :]
        if d < ROWS:
            moved = jnp.concatenate([past.astype(F32)[:, d:, :], moved], 1)
        flow[...] += moved.reshape(N, 128)

    signal_cot[...] = flow[:, 0:RES].astype(BF16).reshape(SEQ, ROWS, RES)
    for tail in range(1, LAYERS + 1):
        for k in range(tail, LAYERS + 1):
            if k - tail < LAYERS:
                stages[k](k - tail)

    for j in range(LAYERS):
        red_wait(red_send.at[0, j], rs_in.at[j])
        if nz > 1:
            red_wait(red_send.at[1, j], part_in.at[j])
            red_wait(red_send.at[3, j], final.at[j, 0, pl.ds(0, nz - 1)])
        if ny > 1:
            red_wait(red_send.at[2, j], line_in.at[j, pl.ds(0, ny - 1)])
        red_wait(red_send.at[4, j], final.at[j, pl.ds(0, GROUP - 1)])


def on_device(ny, nz, signal, skip_grad, stream_grad, w_past, w_now, w_res, w_skip):
    tz = TILES // nz
    scale = 1.0 / math.sqrt(N * 8 * ny * nz)
    vmem = pl.BlockSpec(memory_space=pltpu.VMEM)
    shapes = (
        (SEQ, ROWS, SKIP), (SEQ, ROWS, RES), (SEQ, ROWS, RES),
        (LAYERS, RES, 2 * GATE), (LAYERS, RES, 2 * GATE), (LAYERS, GATE, RES), (LAYERS, GATE, SKIP),
    )
    bf = functools.partial(pltpu.VMEM, dtype=BF16)
    fp = functools.partial(pltpu.VMEM, dtype=F32)
    return pl.pallas_call(
        functools.partial(kernel, ny, nz, scale),
        out_shape=tuple(jax.ShapeDtypeStruct(s, BF16) for s in shapes),
        in_specs=[vmem] * 7,
        out_specs=tuple([vmem] * 7),
        scratch_shapes=[
            bf((LAYERS, 128, 512)),
            bf((LAYERS, 256, 512)),
            bf((LAYERS, 256, 256)),
            bf((LAYERS, 256, 256)),
            fp((LAYERS, SEQ, 256, 128)),
            bf((LAYERS, N, 128)),
            fp((N, 512)),
            bf((N, 256)),
            bf((LAYERS, N, 256)),
            fp((LAYERS, N, 256)),
            fp((LAYERS, N, 256)),
            fp((N, 128)),
            fp((N, 128)),
            fp((N, 256)),
            bf((N, 256)),
            bf((N, 512)),
            bf((SEQ, ROWS, RES)),
            bf((SEQ, ROWS, 128)),
            bf((SEQ, ROWS, 128)),
            bf((LAYERS, SEQ, ROWS, 128)),
            bf((LAYERS, SEQ, ROWS, 128)),
            bf((LAYERS, GROUP, 16, 896)),
            bf((LAYERS, GROUP - 1, 16, 896)),
            bf((LAYERS, nz, tz, 16, 128)),
            bf((LAYERS, max(nz - 1, 1), tz, 16, 128)),
            bf((LAYERS, ny, tz, 16, 128)),
            bf((LAYERS, GROUP, nz, tz, 16, 128)),
            pltpu.SemaphoreType.DMA((7,)),
            pltpu.SemaphoreType.DMA((7,)),
            pltpu.SemaphoreType.DMA((5, LAYERS)),
            pltpu.SemaphoreType.DMA((5, LAYERS)),
        ],
        compiler_params=pltpu.CompilerParams(
            collective_id=0, has_side_effects=True, vmem_limit_bytes=60 * 1024 * 1024
        ),
    )(signal, skip_grad, stream_grad, w_past, w_now, w_res, w_skip)


def solution(mesh):
    blocks = mesh.shape["tm"]
    ny, nz = {128: (8, 8), 4: (1, 2), 8: (2, 2)}[blocks]
    split = P("batch", "tm", None)
    return jax.shard_map(
        functools.partial(on_device, ny, nz),
        mesh=mesh,
        in_specs=(split, split, split, P(), P(), P(), P()),
        out_specs=(split, split, split, P(), P(), P(), P()),
        check_vma=False,
    )
```

```python
import functools
import math

import jax
import jax.numpy as jnp
from jax import lax
from jax.experimental import pallas as pl
from jax.experimental.pallas import tpu as pltpu
from jax.sharding import PartitionSpec as P

MESH = pl.DeviceIdType.MESH
F32 = jnp.float32
BF16 = jnp.bfloat16

RES = 64
GATE = 256
SKIP = 128
LAYERS = 5
SEQ = 4
ROWS = 128
N = SEQ * ROWS
DIL = (8, 16, 32, 64, 128)
LOW = (16, 32, 64, 128, 128)
CHUNK = 32
NX = 4
TILES = 8
WIRE = 7


def nn(left, right):
    return jnp.dot(left, right, preferred_element_type=F32)


def nt(left, right):
    return lax.dot_general(left, right, (((1,), (1,)), ((), ())), preferred_element_type=F32)


def tn(left, right):
    return lax.dot_general(left, right, (((0,), (0,)), ((), ())), preferred_element_type=F32)


def kernel(
    ny, nz, scale,
    signal, skip_grad, stream_grad, w_past, w_now, w_res, w_skip,
    skip_out, stream_out, signal_cot, g_past, g_now, g_res, g_skip,
    sig, sgrad, wres, skipg, skip_st, stream_st, cot_st, past_st, now_st, res_st, gskip_st,
    wx, wb, wf, wg, h2, xs, pre, gat_ext, gated, dfilt, dgate, skip_acc, flow, gcot, flow_b, pcot,
    sig_in, h4_out, h4_in, past_f, past_out, past_in,
    grad, pair_in, half, ring_in, part, part_in, line_in, final,
    load_sem, out_sem, halo_send, halo_recv, red_send, red_recv,
):
    tm = lax.axis_index("tm")
    batch = lax.axis_index("batch")
    blocks = ny * nz * 2
    x_lo = tm % 2
    core = batch % 2
    xi = (batch // 2) * 2 + x_lo
    zi = (tm // 2) % nz
    yi = tm // (2 * nz)
    ei = core * NX + xi
    tz = TILES // nz

    after = {"tm": (tm + 1) % blocks, "batch": batch}
    before = {"tm": (tm + blocks - 1) % blocks, "batch": batch}
    sibling = {"tm": tm, "batch": batch + 1 - 2 * core}
    x_peers = []
    for r in range(1, NX):
        x = (xi + r) % NX
        x_peers.append((x, {"tm": tm - x_lo + x % 2, "batch": (x // 2) * 2 + core}))
    z_peers = []
    for r in range(1, nz):
        z = (zi + r) % nz
        z_peers.append((z, {"tm": (yi * nz + z) * 2 + x_lo, "batch": batch}))
    y_peers = []
    for r in range(1, ny):
        y = (yi + r) % ny
        y_peers.append((y, {"tm": (y * nz + zi) * 2 + x_lo, "batch": batch}))

    barrier = pltpu.get_barrier_semaphore()
    partners = [before, after, sibling] + [peer for _, peer in x_peers + z_peers + y_peers]
    for partner in partners:
        pl.semaphore_signal(barrier, inc=1, device_id=partner, device_id_type=MESH)

    loads = []

    def load(src, dst):
        copy = pltpu.make_async_copy(src, dst, load_sem.at[len(loads)])
        copy.start()
        loads.append(copy)

    load(signal, sig)
    load(w_res, wres)
    load(w_past, wx.at[:, pl.ds(0, 64), :])
    load(w_now, wx.at[:, pl.ds(64, 64), :])
    load(w_skip, wf.at[:, :, pl.ds(0, 128)])
    load(w_skip, wg.at[:, :, pl.ds(0, 128)])
    load(stream_grad, sgrad)
    load(skip_grad, skipg)
    load(w_past, wb.at[:, pl.ds(0, 64), :])
    load(w_past, wb.at[:, pl.ds(64, 64), :])
    load(w_now, wb.at[:, pl.ds(128, 64), :])
    load(w_now, wb.at[:, pl.ds(192, 64), :])

    pl.semaphore_wait(barrier, len(partners))

    def halo_copy(which, src, dst, target):
        return pltpu.make_async_remote_copy(
            src_ref=src, dst_ref=dst, send_sem=halo_send.at[which], recv_sem=halo_recv.at[which],
            device_id=target, device_id_type=MESH,
        )

    first = halo_copy(5, signal, sig_in, after)
    first.start()

    twice = (
        lax.broadcasted_iota(jnp.int32, (RES, 128), 1) % RES
        == lax.broadcasted_iota(jnp.int32, (RES, 128), 0)
    ).astype(F32).astype(BF16)
    once = (
        lax.broadcasted_iota(jnp.int32, (RES, 128), 1)
        == lax.broadcasted_iota(jnp.int32, (RES, 128), 0)
    ).astype(F32).astype(BF16)
    low_half = lax.broadcasted_iota(jnp.int32, (1, 128), 1) < RES
    has_before = jnp.where(tm > 0, 1.0, 0.0).astype(F32)
    has_after = jnp.where(tm < blocks - 1, 1.0, 0.0).astype(F32)
    skip_acc[...] = jnp.zeros_like(skip_acc)
    loads[0].wait()
    for s in range(SEQ):
        h2[0, s, 128:256, :] = tn(sig[s], twice)
    loads[1].wait()
    for j in range(LAYERS):
        both = tn(wres[j], twice)
        wf[j, :, 128:256] = both.astype(BF16)
        wg[j, :, 128:256] = jnp.where(low_half, both, 0.0).astype(BF16)
    for copy in loads[2:]:
        copy.wait()
    for s in range(SEQ):
        flow[s] = tn(sgrad[s], twice)
    first.wait()
    for s in range(SEQ):
        h2[0, s, 0:128, :] = has_before * tn(sig_in[s], twice)

    def gates(j, lo, hi):
        own = lo == 128
        span = hi - lo
        count = SEQ * span
        d = DIL[j]
        x = jnp.where(low_half, h2[j, :, lo - d : hi - d, :], h2[j, :, lo:hi, :])
        x = x.reshape(count, 128).astype(BF16)
        if own:
            xs[j] = x
        pre[0:count, :] = nn(x, wx[j])

        def step(i, carry):
            for u in range(2):
                rows = pl.ds(pl.multiple_of(i * (2 * CHUNK) + u * CHUNK, CHUNK), CHUNK)
                t = jnp.tanh(pre[rows, 0:GATE])
                s = 0.5 * jnp.tanh(0.5 * pre[rows, GATE : 2 * GATE]) + 0.5
                ts = t * s
                if own:
                    gated[j, rows, :] = ts.astype(BF16)
                    dfilt[j, rows, :] = s * (1.0 - t * t)
                    dgate[j, rows, :] = ts * (1.0 - s)
                else:
                    gat_ext[rows, :] = ts.astype(BF16)
            return carry

        lax.fori_loop(0, count // (2 * CHUNK), step, 0)

    def advance(j, lo, hi):
        own = lo == 128
        span = hi - lo
        count = SEQ * span
        y = nn(gated[j] if own else gat_ext[0:count, :], wf[j])
        if own:
            skip_acc[...] += y[:, 0:128]
        new = h2[j, :, lo:hi, :].reshape(count, 128) + y[:, 128:256]
        new = new.astype(BF16)
        if j + 1 < LAYERS:
            h2[j + 1, :, lo:hi, :] = new.astype(F32).reshape(SEQ, span, 128)
        return new

    for j in range(4):
        if LOW[j] < 128:
            gates(j, LOW[j], 128)
            advance(j, LOW[j], 128)
        gates(j, 128, 256)
        new = advance(j, 128, 256)
    h4_out[...] = new.reshape(SEQ, ROWS, 128)
    second = halo_copy(6, h4_out, h4_in, after)
    second.start()

    def cotangent(j, a, b):
        count = SEQ * (b - a)
        fb = flow[:, a:b, :].astype(BF16)
        flow_b[j, :, a:b, :] = fb
        left = jnp.concatenate([skipg[:, a:b, :], fb], 2).reshape(count, 256)
        gcot[0:count, :] = nt(left, wg[j])

    def back(j, a, b):
        span = b - a
        count = SEQ * span
        size = CHUNK if span % CHUNK == 0 else 16
        per = span // size

        def step(i, carry):
            s = i // per
            here = pl.ds(pl.multiple_of(i * size, 16), size)
            rows = pl.ds(pl.multiple_of(a + (i % per) * size, 16), size)
            flat = pl.ds(pl.multiple_of(s * ROWS + a + (i % per) * size, 16), size)
            gc = gcot[here, :]
            pcot[j, s, rows, 0:GATE] = (gc * dfilt[j, flat, :]).astype(BF16)
            pcot[j, s, rows, GATE : 2 * GATE] = (gc * dgate[j, flat, :]).astype(BF16)
            return carry

        lax.fori_loop(0, SEQ * per, step, 0)
        both = nt(pcot[j, :, a:b, :].reshape(count, 2 * GATE), wb[j])
        past = both[:, 0:128].astype(BF16).reshape(SEQ, span, 128)
        past_out[j, :, a:b, :] = past
        past_f[j, :, a:b, :] = past.astype(F32)
        flow[:, a:b, :] += both[:, 128:256].reshape(SEQ, span, 128)

    def head_copy(j):
        rows = pl.ds(0, max(DIL[j], 16))
        return halo_copy(j, past_out.at[j, :, rows, :], past_in.at[j, :, rows, :], before)

    def move(j, a, b):
        d = DIL[j]
        lo, hi = a + d, b + d
        pieces = []
        if lo < ROWS:
            pieces.append(past_f[j, :, lo : min(hi, ROWS), :])
        if hi > ROWS:
            edge = past_in[j, :, 0 : max(d, 16), :].astype(F32)
            pieces.append(has_after * edge[:, max(lo - ROWS, 0) : hi - ROWS, :])
        flow[:, a:b, :] += pieces[0] if len(pieces) == 1 else jnp.concatenate(pieces, 1)

    def weight_sums(j):
        gx = tn(xs[j], pcot[j].reshape(N, 2 * GATE))
        right = jnp.concatenate([skipg[...], flow_b[j]], 2).reshape(N, 256)
        gy = tn(gated[j], right)
        grad[j, :, :, 0:512] = gx.astype(BF16).reshape(2 * NX, 16, 512)
        packed = jnp.where(low_half, gy[0:128, 128:256], gy[128:256, 128:256]).T
        grad[j, :, :, 512:640] = packed.astype(BF16).reshape(2 * NX, 16, 128)
        grad[j, :, :, 640:768] = gy[0:128, 0:128].astype(BF16).reshape(2 * NX, 16, 128)
        grad[j, :, :, 768:896] = gy[128:256, 0:128].astype(BF16).reshape(2 * NX, 16, 128)

    def red_copy(stage, j, src, dst, target):
        pltpu.make_async_remote_copy(
            src_ref=src, dst_ref=dst, send_sem=red_send.at[stage, j], recv_sem=red_recv.at[stage, j],
            device_id=target, device_id_type=MESH,
        ).start()

    def red_wait(sem, ref):
        pltpu.make_async_copy(ref, ref, sem).wait()

    mine = pl.ds(core * NX, NX)
    other = pl.ds((1 - core) * NX, NX)

    def scatter_core(j):
        red_copy(0, j, grad.at[j, other], pair_in.at[j], sibling)

    def scatter_x(j):
        red_wait(red_recv.at[0, j], pair_in.at[j])
        half[j] = (grad[j, mine].astype(F32) + pair_in[j].astype(F32)).astype(BF16)
        for r, (x, peer) in enumerate(x_peers):
            red_copy(1, j, half.at[j, x], ring_in.at[j, r], peer)

    def scatter_z(j):
        red_wait(red_recv.at[1, j], ring_in.at[j])
        total = half[j, xi].astype(F32)
        for r in range(NX - 1):
            total += ring_in[j, r].astype(F32)
        for k in range(WIRE):
            part[j, k // tz, k % tz] = total[:, 128 * k : 128 * k + 128].astype(BF16)
        for k in range(WIRE, TILES):
            part[j, k // tz, k % tz] = jnp.zeros((16, 128), BF16)
        for r, (z, peer) in enumerate(z_peers):
            red_copy(2, j, part.at[j, z], part_in.at[j, r], peer)

    def across_y(j):
        if nz > 1:
            red_wait(red_recv.at[2, j], part_in.at[j])
        total = part[j, zi].astype(F32)
        for r in range(nz - 1):
            total += part_in[j, r].astype(F32)
        line_in[j, yi] = total.astype(BF16)
        for _, peer in y_peers:
            red_copy(3, j, line_in.at[j, yi], line_in.at[j, yi], peer)

    def gather_z(j):
        if ny > 1:
            red_wait(red_recv.at[3, j], line_in.at[j, pl.ds(0, ny - 1)])
        total = line_in[j, 0].astype(F32)
        for r in range(1, ny):
            total += line_in[j, r].astype(F32)
        final[j, ei, zi] = (total * scale).astype(BF16)
        for _, peer in z_peers:
            red_copy(4, j, final.at[j, ei, zi], final.at[j, ei, zi], peer)

    def gather_x(j):
        if nz > 1:
            red_wait(red_recv.at[4, j], final.at[j, 0, pl.ds(0, nz - 1)])
        for _, peer in x_peers:
            red_copy(5, j, final.at[j, ei], final.at[j, ei], peer)

    def gather_core(j):
        red_wait(red_recv.at[5, j], final.at[j, pl.ds(0, NX - 1)])
        red_copy(6, j, final.at[j, mine], final.at[j, mine], sibling)

    def store(which, src, dst):
        pltpu.make_async_copy(src, dst, out_sem.at[which]).start()

    def finish(j):
        red_wait(red_recv.at[6, j], final.at[j, pl.ds(0, NX)])
        tile = [final[j, :, k // tz, k % tz].reshape(128, 128) for k in range(WIRE)]
        for k in range(4):
            past_st[j, :, 128 * k : 128 * k + 128] = tile[k][0:64]
            now_st[j, :, 128 * k : 128 * k + 128] = tile[k][64:128]
        res_st[j, :, 0:128] = tile[4][0:64]
        res_st[j, :, 128:256] = tile[4][64:128]
        gskip_st[j, 0:128, :] = tile[5]
        gskip_st[j, 128:256, :] = tile[6]
        store(3, past_st.at[j], g_past.at[j])
        store(4, now_st.at[j], g_now.at[j])
        store(5, res_st.at[j], g_res.at[j])
        store(6, gskip_st.at[j], g_skip.at[j])

    stages = (
        scatter_core, scatter_x, scatter_z, across_y, gather_z, gather_x, gather_core, finish
    )

    def turn(*work):
        for k, j in work:
            stages[k](j)

    cotangent(4, 0, ROWS)
    second.wait()
    h2[4, :, 0:128, :] = has_before * h4_in[...].astype(F32)
    gates(4, 128, 256)
    heads = [head_copy(j) for j in range(LAYERS)]
    back(4, 0, ROWS)
    heads[4].start()
    new = advance(4, 128, 256)
    for s in range(SEQ):
        stream_st[s] = nt(once, new[s * ROWS : (s + 1) * ROWS]).astype(BF16)
    skip_st[...] = skip_acc[...].astype(BF16).reshape(SEQ, ROWS, SKIP)
    store(0, skip_st, skip_out)
    store(1, stream_st, stream_out)
    weight_sums(4)
    turn((0, 4))

    heads[4].wait()
    move(4, 0, ROWS)
    cotangent(3, 0, ROWS)
    back(3, 0, ROWS)
    heads[3].start()
    for j in (3, 2, 1):
        d = DIL[j]
        move(j, 0, d)
        cotangent(j - 1, 0, d)
        back(j - 1, 0, d)
        heads[j - 1].start()
    weight_sums(3)
    turn((0, 3), (1, 4))
    during = {
        3: ((0, 2), (1, 3)),
        2: ((0, 1), (1, 2), (2, 4)),
        1: ((0, 0), (1, 1), (1, 0), (2, 3), (2, 2), (3, 4)),
    }
    for j in (3, 2, 1):
        d = DIL[j]
        heads[j].wait()
        move(j, d, ROWS)
        cotangent(j - 1, d, ROWS)
        back(j - 1, d, ROWS)
        weight_sums(j - 1)
        turn(*during[j])
    heads[0].wait()
    move(0, 0, ROWS)
    for s in range(SEQ):
        cot_st[s] = nt(once, flow[s].astype(BF16)).astype(BF16)
    store(2, cot_st, signal_cot)
    for k in range(2, len(stages)):
        turn((k, 0), (k, 1))
        if k + 1 < len(stages):
            turn((k + 1, 3), (k + 1, 2))
        if k + 2 < len(stages):
            turn((k + 2, 4))

    for j in range(LAYERS):
        red_wait(red_send.at[0, j], pair_in.at[j])
        red_wait(red_send.at[1, j], ring_in.at[j])
        if nz > 1:
            red_wait(red_send.at[2, j], part_in.at[j])
            red_wait(red_send.at[4, j], final.at[j, 0, pl.ds(0, nz - 1)])
        if ny > 1:
            red_wait(red_send.at[3, j], line_in.at[j, pl.ds(0, ny - 1)])
        red_wait(red_send.at[5, j], final.at[j, pl.ds(0, NX - 1)])
        red_wait(red_send.at[6, j], final.at[j, pl.ds(0, NX)])
    staged = (skip_st, stream_st, cot_st, past_st, now_st, res_st, gskip_st)
    outs = (skip_out, stream_out, signal_cot, g_past, g_now, g_res, g_skip)
    for which in range(7):
        pltpu.make_async_copy(staged[which], outs[which], out_sem.at[which]).wait()


def relay(*refs):
    ins, outs, held, in_sem, out_sem = refs[:7], refs[7:14], refs[14:21], refs[21], refs[22]
    loads = [pltpu.make_async_copy(ins[i], held[i], in_sem.at[i]) for i in range(7)]
    stores = [pltpu.make_async_copy(held[i], outs[i], out_sem.at[i]) for i in range(7)]
    for copy in loads:
        copy.start()
    for i in range(7):
        loads[i].wait()
        stores[i].start()
    for copy in stores:
        copy.wait()


def on_device(ny, nz, signal, skip_grad, stream_grad, w_past, w_now, w_res, w_skip):
    tz = TILES // nz
    scale = 1.0 / math.sqrt(N * 8 * ny * nz)
    shapes = (
        (SEQ, ROWS, SKIP), (SEQ, RES, ROWS), (SEQ, RES, ROWS),
        (LAYERS, RES, 2 * GATE), (LAYERS, RES, 2 * GATE), (LAYERS, RES, GATE), (LAYERS, GATE, SKIP),
    )
    anywhere = pl.BlockSpec(memory_space=pl.ANY)
    results = tuple(jax.ShapeDtypeStruct(s, BF16) for s in shapes)
    bf = functools.partial(pltpu.VMEM, dtype=BF16)
    fp = functools.partial(pltpu.VMEM, dtype=F32)
    outs = pl.pallas_call(
        functools.partial(kernel, ny, nz, scale),
        out_shape=results,
        in_specs=[anywhere] * 7,
        out_specs=(anywhere,) * 7,
        scratch_shapes=[
            bf((SEQ, RES, ROWS)),
            bf((SEQ, RES, ROWS)),
            bf((LAYERS, RES, GATE)),
            bf((SEQ, ROWS, SKIP)),
            *[bf(s) for s in shapes],
            bf((LAYERS, 128, 512)),
            bf((LAYERS, 256, 512)),
            bf((LAYERS, 256, 256)),
            bf((LAYERS, 256, 256)),
            fp((LAYERS, SEQ, 256, 128)),
            bf((LAYERS, N, 128)),
            fp((N, 512)),
            bf((N, 256)),
            bf((LAYERS, N, 256)),
            fp((LAYERS, N, 256)),
            fp((LAYERS, N, 256)),
            fp((N, 128)),
            fp((SEQ, ROWS, 128)),
            fp((N, 256)),
            bf((LAYERS, SEQ, ROWS, 128)),
            bf((LAYERS, SEQ, ROWS, 512)),
            bf((SEQ, RES, ROWS)),
            bf((SEQ, ROWS, 128)),
            bf((SEQ, ROWS, 128)),
            fp((LAYERS, SEQ, ROWS, 128)),
            bf((LAYERS, SEQ, ROWS, 128)),
            bf((LAYERS, SEQ, ROWS, 128)),
            bf((LAYERS, 2 * NX, 16, 896)),
            bf((LAYERS, NX, 16, 896)),
            bf((LAYERS, NX, 16, 896)),
            bf((LAYERS, NX - 1, 16, 896)),
            bf((LAYERS, nz, tz, 16, 128)),
            bf((LAYERS, max(nz - 1, 1), tz, 16, 128)),
            bf((LAYERS, ny, tz, 16, 128)),
            bf((LAYERS, 2 * NX, nz, tz, 16, 128)),
            pltpu.SemaphoreType.DMA((12,)),
            pltpu.SemaphoreType.DMA((7,)),
            pltpu.SemaphoreType.DMA((7,)),
            pltpu.SemaphoreType.DMA((7,)),
            pltpu.SemaphoreType.DMA((7, LAYERS)),
            pltpu.SemaphoreType.DMA((7, LAYERS)),
        ],
        compiler_params=pltpu.CompilerParams(
            collective_id=0, has_side_effects=True, vmem_limit_bytes=60 * 1024 * 1024
        ),
    )(
        jnp.swapaxes(signal, 1, 2), skip_grad, jnp.swapaxes(stream_grad, 1, 2),
        w_past, w_now, jnp.swapaxes(w_res, 1, 2), w_skip,
    )
    outs = pl.pallas_call(
        relay,
        out_shape=results,
        in_specs=[anywhere] * 7,
        out_specs=(anywhere,) * 7,
        scratch_shapes=[*[bf(s) for s in shapes]] + [pltpu.SemaphoreType.DMA((7,))] * 2,
    )(*outs)
    skip, stream, cot, g_past, g_now, g_res, g_skip = outs
    return (
        skip, jnp.swapaxes(stream, 1, 2), jnp.swapaxes(cot, 1, 2),
        g_past, g_now, jnp.swapaxes(g_res, 1, 2), g_skip,
    )


def solution(mesh):
    blocks = mesh.shape["tm"]
    ny, nz = {128: (8, 8), 4: (1, 2), 8: (2, 2)}[blocks]
    split = P("batch", "tm", None)
    return jax.shard_map(
        functools.partial(on_device, ny, nz),
        mesh=mesh,
        in_specs=(split, split, split, P(), P(), P(), P()),
        out_specs=(split, split, split, P(), P(), P(), P()),
        check_vma=False,
    )
```

```python
import functools
import math

import jax
import jax.numpy as jnp
from jax import lax
from jax.experimental import pallas as pl
from jax.experimental.pallas import tpu as pltpu
from jax.sharding import PartitionSpec as P

MESH = pl.DeviceIdType.MESH
F32 = jnp.float32
BF16 = jnp.bfloat16

RES = 64
GATE = 256
SKIP = 128
LAYERS = 5
SEQ = 4
ROWS = 128
N = SEQ * ROWS
DIL = (8, 16, 32, 64, 128)
LOW = (16, 32, 64, 128, 128)
CHUNK = 32
NX = 4
TILES = 8
WIRE = 7


def nn(left, right):
    return jnp.dot(left, right, preferred_element_type=F32)


def nt(left, right):
    return lax.dot_general(left, right, (((1,), (1,)), ((), ())), preferred_element_type=F32)


def tn(left, right):
    return lax.dot_general(left, right, (((0,), (0,)), ((), ())), preferred_element_type=F32)


def far_first(n):
    return sorted(range(1, n), key=lambda r: -min(r, n - r))


def kernel(
    ny, nz, scale,
    signal, skip_grad, stream_grad, w_past, w_now, w_res, w_skip,
    skip_st, stream_st, cot_st, past_st, now_st, res_st, gskip_st,
    sig, sgrad, wres, skipg,
    wx, wb, wf, wg, h2, xs, pre, gated, dfilt, dgate, skip_acc, flow, gcot, flow_b, pcot,
    sig_in, h4_out, h4_in, past_f, past_out, past_in,
    grad, pair_in, half, ring_in, part, part_in, line_in, final,
    load_sem, halo_send, halo_recv, red_send, red_recv,
):
    tm = lax.axis_index("tm")
    batch = lax.axis_index("batch")
    blocks = ny * nz * 2
    x_lo = tm % 2
    core = batch % 2
    xi = (batch // 2) * 2 + x_lo
    zi = (tm // 2) % nz
    yi = tm // (2 * nz)
    ei = core * NX + xi
    tz = TILES // nz

    after = {"tm": (tm + 1) % blocks, "batch": batch}
    before = {"tm": (tm + blocks - 1) % blocks, "batch": batch}
    sibling = {"tm": tm, "batch": batch + 1 - 2 * core}
    x_peers = []
    for r in far_first(NX):
        x = (xi + r) % NX
        x_peers.append((x, {"tm": tm - x_lo + x % 2, "batch": (x // 2) * 2 + core}))
    z_peers = []
    for r in far_first(nz):
        z = (zi + r) % nz
        z_peers.append((z, {"tm": (yi * nz + z) * 2 + x_lo, "batch": batch}))
    y_peers = []
    for r in far_first(ny):
        y = (yi + r) % ny
        y_peers.append((y, {"tm": (y * nz + zi) * 2 + x_lo, "batch": batch}))

    barrier = pltpu.get_barrier_semaphore()
    partners = [before, after, sibling] + [peer for _, peer in x_peers + z_peers + y_peers]
    for partner in partners:
        pl.semaphore_signal(barrier, inc=1, device_id=partner, device_id_type=MESH)

    loads = []

    def load(src, dst):
        copy = pltpu.make_async_copy(src, dst, load_sem.at[len(loads)])
        copy.start()
        loads.append(copy)

    load(signal, sig)
    load(w_res, wres)
    load(w_past, wx.at[:, pl.ds(0, 64), :])
    load(w_now, wx.at[:, pl.ds(64, 64), :])
    load(w_skip, wf.at[:, :, pl.ds(0, 128)])
    load(w_skip, wg.at[:, :, pl.ds(0, 128)])
    load(stream_grad, sgrad)
    load(skip_grad, skipg)
    load(w_past, wb.at[:, pl.ds(0, 64), :])
    load(w_past, wb.at[:, pl.ds(64, 64), :])
    load(w_now, wb.at[:, pl.ds(128, 64), :])
    load(w_now, wb.at[:, pl.ds(192, 64), :])

    pl.semaphore_wait(barrier, len(partners))

    def halo_copy(which, src, dst, target):
        return pltpu.make_async_remote_copy(
            src_ref=src, dst_ref=dst, send_sem=halo_send.at[which], recv_sem=halo_recv.at[which],
            device_id=target, device_id_type=MESH,
        )

    first = halo_copy(5, signal, sig_in, after)
    first.start()

    twice = (
        lax.broadcasted_iota(jnp.int32, (RES, 128), 1) % RES
        == lax.broadcasted_iota(jnp.int32, (RES, 128), 0)
    ).astype(F32).astype(BF16)
    once = (
        lax.broadcasted_iota(jnp.int32, (RES, 128), 1)
        == lax.broadcasted_iota(jnp.int32, (RES, 128), 0)
    ).astype(F32).astype(BF16)
    low_half = lax.broadcasted_iota(jnp.int32, (1, 128), 1) < RES
    has_before = jnp.where(tm > 0, 1.0, 0.0).astype(F32)
    has_after = jnp.where(tm < blocks - 1, 1.0, 0.0).astype(F32)
    skip_acc[...] = jnp.zeros_like(skip_acc)
    loads[0].wait()
    for s in range(SEQ):
        h2[0, s, 128:256, :] = tn(sig[s], twice)
    loads[1].wait()
    for j in range(LAYERS):
        both = tn(wres[j], twice)
        wf[j, :, 128:256] = both.astype(BF16)
        wg[j, :, 128:256] = jnp.where(low_half, both, 0.0).astype(BF16)
    for copy in loads[2:]:
        copy.wait()
    for s in range(SEQ):
        flow[s] = tn(sgrad[s], twice)

    def gates(j, lo, hi):
        span = hi - lo
        count = SEQ * span
        d = DIL[j]
        size = CHUNK if span % CHUNK == 0 else 16
        own = max(lo, 128)
        x = jnp.where(low_half, h2[j, :, lo - d : hi - d, :], h2[j, :, lo:hi, :]).astype(BF16)
        xs[j, :, own - 128 : hi - 128, :] = x[:, own - lo :, :]
        pre[0:count, :] = nn(x.reshape(count, 128), wx[j])

        def step(q, carry):
            for c in range(0, span, size):
                rows = pl.ds(pl.multiple_of(q * span + c, 16), size)
                t = jnp.tanh(pre[rows, 0:GATE])
                s = 0.5 * jnp.tanh(0.5 * pre[rows, GATE : 2 * GATE]) + 0.5
                ts = t * s
                gated[j, q, lo + c : lo + c + size, :] = ts.astype(BF16)
                if lo + c + size > 128:
                    dfilt[j, q, lo + c : lo + c + size, :] = s * (1.0 - t * t)
                    dgate[j, q, lo + c : lo + c + size, :] = ts * (1.0 - s)
            return carry

        lax.fori_loop(0, SEQ, step, 0)

    def advance(j, lo, hi):
        span = hi - lo
        count = SEQ * span
        own = max(lo, 128)
        y = nn(gated[j, :, lo:hi, :].reshape(count, GATE), wf[j]).reshape(SEQ, span, 256)
        skip_acc[:, own - 128 : hi - 128, :] += y[:, own - lo :, 0:128]
        new = (h2[j, :, lo:hi, :] + y[:, :, 128:256]).astype(BF16)
        if j + 1 < LAYERS:
            h2[j + 1, :, lo:hi, :] = new.astype(F32)
        return new

    for j in range(3):
        gates(j, LOW[j] + 128, 256)
        advance(j, LOW[j] + 128, 256)
    first.wait()
    for s in range(SEQ):
        h2[0, s, 0:128, :] = has_before * tn(sig_in[s], twice)
    for j in range(3):
        gates(j, LOW[j], LOW[j] + 128)
        advance(j, LOW[j], LOW[j] + 128)
    gates(3, 128, 256)
    new = advance(3, 128, 256)
    h4_out[...] = new
    second = halo_copy(6, h4_out, h4_in, after)
    second.start()

    def cotangent(j, a, b):
        count = SEQ * (b - a)
        fb = flow[:, a:b, :].astype(BF16)
        flow_b[j, :, a:b, :] = fb
        left = jnp.concatenate([skipg[:, a:b, :], fb], 2).reshape(count, 256)
        gcot[0:count, :] = nt(left, wg[j])

    def back(j, a, b):
        span = b - a
        count = SEQ * span
        size = CHUNK if span % CHUNK == 0 else 16
        per = span // size

        def step(i, carry):
            s = i // per
            here = pl.ds(pl.multiple_of(i * size, 16), size)
            rows = pl.ds(pl.multiple_of(a + (i % per) * size, 16), size)
            held = pl.ds(pl.multiple_of(128 + a + (i % per) * size, 16), size)
            gc = gcot[here, :]
            pcot[j, s, rows, 0:GATE] = (gc * dfilt[j, s, held, :]).astype(BF16)
            pcot[j, s, rows, GATE : 2 * GATE] = (gc * dgate[j, s, held, :]).astype(BF16)
            return carry

        lax.fori_loop(0, SEQ * per, step, 0)
        both = nt(pcot[j, :, a:b, :].reshape(count, 2 * GATE), wb[j])
        past = both[:, 0:128].astype(BF16).reshape(SEQ, span, 128)
        past_out[j, :, a:b, :] = past
        past_f[j, :, a:b, :] = past.astype(F32)
        flow[:, a:b, :] += both[:, 128:256].reshape(SEQ, span, 128)

    def head_copy(j):
        rows = pl.ds(0, max(DIL[j], 16))
        return halo_copy(j, past_out.at[j, :, rows, :], past_in.at[j, :, rows, :], before)

    def move(j, a, b):
        d = DIL[j]
        lo, hi = a + d, b + d
        pieces = []
        if lo < ROWS:
            pieces.append(past_f[j, :, lo : min(hi, ROWS), :])
        if hi > ROWS:
            edge = past_in[j, :, 0 : max(d, 16), :].astype(F32)
            pieces.append(has_after * edge[:, max(lo - ROWS, 0) : hi - ROWS, :])
        flow[:, a:b, :] += pieces[0] if len(pieces) == 1 else jnp.concatenate(pieces, 1)

    def weight_sums(j):
        gx = tn(xs[j].reshape(N, 128), pcot[j].reshape(N, 2 * GATE))
        right = jnp.concatenate([skipg[...], flow_b[j]], 2).reshape(N, 256)
        gy = tn(gated[j, :, 128:256, :].reshape(N, GATE), right)
        grad[j, :, :, 0:512] = gx.astype(BF16).reshape(2 * NX, 16, 512)
        packed = jnp.where(low_half, gy[0:128, 128:256], gy[128:256, 128:256]).T
        grad[j, :, :, 512:640] = packed.astype(BF16).reshape(2 * NX, 16, 128)
        grad[j, :, :, 640:768] = gy[0:128, 0:128].astype(BF16).reshape(2 * NX, 16, 128)
        grad[j, :, :, 768:896] = gy[128:256, 0:128].astype(BF16).reshape(2 * NX, 16, 128)

    def red_copy(stage, j, src, dst, target):
        pltpu.make_async_remote_copy(
            src_ref=src, dst_ref=dst, send_sem=red_send.at[stage, j], recv_sem=red_recv.at[stage, j],
            device_id=target, device_id_type=MESH,
        ).start()

    def red_wait(sem, ref):
        pltpu.make_async_copy(ref, ref, sem).wait()

    mine = pl.ds(core * NX, NX)
    other = pl.ds((1 - core) * NX, NX)

    def scatter_core(j):
        red_copy(0, j, grad.at[j, other], pair_in.at[j], sibling)

    def scatter_x(j):
        red_wait(red_recv.at[0, j], pair_in.at[j])
        half[j] = (grad[j, mine].astype(F32) + pair_in[j].astype(F32)).astype(BF16)
        for r, (x, peer) in enumerate(x_peers):
            red_copy(1, j, half.at[j, x], ring_in.at[j, r], peer)

    def scatter_z(j):
        red_wait(red_recv.at[1, j], ring_in.at[j])
        total = half[j, xi].astype(F32)
        for r in range(NX - 1):
            total += ring_in[j, r].astype(F32)
        for k in range(WIRE):
            part[j, k // tz, k % tz] = total[:, 128 * k : 128 * k + 128].astype(BF16)
        for k in range(WIRE, TILES):
            part[j, k // tz, k % tz] = jnp.zeros((16, 128), BF16)
        for r, (z, peer) in enumerate(z_peers):
            red_copy(2, j, part.at[j, z], part_in.at[j, r], peer)

    def across_y(j):
        if nz > 1:
            red_wait(red_recv.at[2, j], part_in.at[j])
        total = part[j, zi].astype(F32)
        for r in range(nz - 1):
            total += part_in[j, r].astype(F32)
        line_in[j, yi] = total.astype(BF16)
        for _, peer in y_peers:
            red_copy(3, j, line_in.at[j, yi], line_in.at[j, yi], peer)

    def gather_z(j):
        if ny > 1:
            red_wait(red_recv.at[3, j], line_in.at[j, pl.ds(0, ny - 1)])
        total = line_in[j, 0].astype(F32)
        for r in range(1, ny):
            total += line_in[j, r].astype(F32)
        final[j, ei, zi] = (total * scale).astype(BF16)
        for _, peer in z_peers:
            red_copy(4, j, final.at[j, ei, zi], final.at[j, ei, zi], peer)

    def gather_x(j):
        if nz > 1:
            red_wait(red_recv.at[4, j], final.at[j, 0, pl.ds(0, nz - 1)])
        for _, peer in x_peers:
            red_copy(5, j, final.at[j, ei], final.at[j, ei], peer)

    def gather_core(j):
        red_wait(red_recv.at[5, j], final.at[j, pl.ds(0, NX - 1)])
        red_copy(6, j, final.at[j, mine], final.at[j, mine], sibling)

    def finish(j):
        red_wait(red_recv.at[6, j], final.at[j, pl.ds(0, NX)])
        tile = [final[j, :, k // tz, k % tz].reshape(128, 128) for k in range(WIRE)]
        for k in range(4):
            past_st[j, :, 128 * k : 128 * k + 128] = tile[k][0:64]
            now_st[j, :, 128 * k : 128 * k + 128] = tile[k][64:128]
        res_st[j, :, 0:128] = tile[4][0:64]
        res_st[j, :, 128:256] = tile[4][64:128]
        gskip_st[j, 0:128, :] = tile[5]
        gskip_st[j, 128:256, :] = tile[6]

    stages = (
        scatter_core, scatter_x, scatter_z, across_y, gather_z, gather_x, gather_core, finish
    )

    def turn(*work):
        for k, j in work:
            stages[k](j)

    cotangent(4, 0, ROWS)
    second.wait()
    h2[4, :, 0:128, :] = has_before * h4_in[...].astype(F32)
    gates(4, 128, 256)
    heads = [head_copy(j) for j in range(LAYERS)]
    back(4, 0, ROWS)
    heads[4].start()
    new = advance(4, 128, 256)
    for s in range(SEQ):
        stream_st[s] = nt(once, new[s]).astype(BF16)
    skip_st[...] = skip_acc[...].astype(BF16)
    weight_sums(4)
    turn((0, 4))

    heads[4].wait()
    move(4, 0, ROWS)
    cotangent(3, 0, DIL[3])
    back(3, 0, DIL[3])
    heads[3].start()
    cotangent(3, DIL[3], ROWS)
    back(3, DIL[3], ROWS)
    for j in (3, 2, 1):
        d = DIL[j]
        move(j, 0, d)
        cotangent(j - 1, 0, d)
        back(j - 1, 0, d)
        heads[j - 1].start()
    weight_sums(3)
    turn((0, 3), (1, 4))
    during = {
        3: ((0, 2), (1, 3)),
        2: ((0, 1), (1, 2), (2, 4)),
        1: ((0, 0), (1, 1), (1, 0), (2, 3), (2, 2), (3, 4)),
    }
    for j in (3, 2, 1):
        d = DIL[j]
        heads[j].wait()
        move(j, d, ROWS)
        cotangent(j - 1, d, ROWS)
        back(j - 1, d, ROWS)
        weight_sums(j - 1)
        turn(*during[j])
    heads[0].wait()
    move(0, 0, ROWS)
    for s in range(SEQ):
        cot_st[s] = nt(once, flow[s].astype(BF16)).astype(BF16)
    for k in range(2, len(stages)):
        turn((k, 0), (k, 1))
        if k + 1 < len(stages):
            turn((k + 1, 3), (k + 1, 2))
        if k + 2 < len(stages):
            turn((k + 2, 4))

    for j in range(LAYERS):
        red_wait(red_send.at[0, j], pair_in.at[j])
        red_wait(red_send.at[1, j], ring_in.at[j])
        if nz > 1:
            red_wait(red_send.at[2, j], part_in.at[j])
            red_wait(red_send.at[4, j], final.at[j, 0, pl.ds(0, nz - 1)])
        if ny > 1:
            red_wait(red_send.at[3, j], line_in.at[j, pl.ds(0, ny - 1)])
        red_wait(red_send.at[5, j], final.at[j, pl.ds(0, NX - 1)])
        red_wait(red_send.at[6, j], final.at[j, pl.ds(0, NX)])


def relay(*refs):
    copies = [pltpu.make_async_copy(refs[i], refs[7 + i], refs[14].at[i]) for i in range(7)]
    for copy in copies:
        copy.start()
    for copy in copies:
        copy.wait()


def on_device(ny, nz, signal, skip_grad, stream_grad, w_past, w_now, w_res, w_skip):
    tz = TILES // nz
    scale = 1.0 / math.sqrt(N * 8 * ny * nz)
    shapes = (
        (SEQ, ROWS, SKIP), (SEQ, RES, ROWS), (SEQ, RES, ROWS),
        (LAYERS, RES, 2 * GATE), (LAYERS, RES, 2 * GATE), (LAYERS, RES, GATE), (LAYERS, GATE, SKIP),
    )
    hbm = pl.BlockSpec(memory_space=pltpu.HBM)
    vmem = pl.BlockSpec(memory_space=pltpu.VMEM)
    bf = functools.partial(pltpu.VMEM, dtype=BF16)
    fp = functools.partial(pltpu.VMEM, dtype=F32)
    outs = pl.pallas_call(
        functools.partial(kernel, ny, nz, scale),
        out_shape=tuple(pltpu.VMEM(s, BF16) for s in shapes),
        in_specs=[hbm] * 7,
        out_specs=(vmem,) * 7,
        scratch_shapes=[
            bf((SEQ, RES, ROWS)),
            bf((SEQ, RES, ROWS)),
            bf((LAYERS, RES, GATE)),
            bf((SEQ, ROWS, SKIP)),
            bf((LAYERS, 128, 512)),
            bf((LAYERS, 256, 512)),
            bf((LAYERS, 256, 256)),
            bf((LAYERS, 256, 256)),
            fp((LAYERS, SEQ, 256, 128)),
            bf((LAYERS, SEQ, ROWS, 128)),
            fp((N, 512)),
            bf((LAYERS, SEQ, 256, 256)),
            fp((LAYERS, SEQ, 256, 256)),
            fp((LAYERS, SEQ, 256, 256)),
            fp((SEQ, ROWS, 128)),
            fp((SEQ, ROWS, 128)),
            fp((N, 256)),
            bf((LAYERS, SEQ, ROWS, 128)),
            bf((LAYERS, SEQ, ROWS, 512)),
            bf((SEQ, RES, ROWS)),
            bf((SEQ, ROWS, 128)),
            bf((SEQ, ROWS, 128)),
            fp((LAYERS, SEQ, ROWS, 128)),
            bf((LAYERS, SEQ, ROWS, 128)),
            bf((LAYERS, SEQ, ROWS, 128)),
            bf((LAYERS, 2 * NX, 16, 896)),
            bf((LAYERS, NX, 16, 896)),
            bf((LAYERS, NX, 16, 896)),
            bf((LAYERS, NX - 1, 16, 896)),
            bf((LAYERS, nz, tz, 16, 128)),
            bf((LAYERS, max(nz - 1, 1), tz, 16, 128)),
            bf((LAYERS, ny, tz, 16, 128)),
            bf((LAYERS, 2 * NX, nz, tz, 16, 128)),
            pltpu.SemaphoreType.DMA((12,)),
            pltpu.SemaphoreType.DMA((7,)),
            pltpu.SemaphoreType.DMA((7,)),
            pltpu.SemaphoreType.DMA((7, LAYERS)),
            pltpu.SemaphoreType.DMA((7, LAYERS)),
        ],
        compiler_params=pltpu.CompilerParams(
            collective_id=0, has_side_effects=True, vmem_limit_bytes=44 * 1024 * 1024
        ),
    )(
        *(
            pltpu.with_memory_space_constraint(array, pltpu.HBM)
            for array in (
                jnp.swapaxes(signal, 1, 2), skip_grad, jnp.swapaxes(stream_grad, 1, 2),
                w_past, w_now, jnp.swapaxes(w_res, 1, 2), w_skip,
            )
        )
    )
    outs = pl.pallas_call(
        relay,
        out_shape=tuple(pltpu.HBM(s, BF16) for s in shapes),
        in_specs=[vmem] * 7,
        out_specs=(hbm,) * 7,
        scratch_shapes=[pltpu.SemaphoreType.DMA((7,))],
        compiler_params=pltpu.CompilerParams(vmem_limit_bytes=16 * 1024 * 1024),
    )(*(pltpu.with_memory_space_constraint(array, pltpu.VMEM) for array in outs))
    skip, stream, cot, g_past, g_now, g_res, g_skip = outs
    return (
        skip, jnp.swapaxes(stream, 1, 2), jnp.swapaxes(cot, 1, 2),
        g_past, g_now, jnp.swapaxes(g_res, 1, 2), g_skip,
    )


def solution(mesh):
    blocks = mesh.shape["tm"]
    ny, nz = {128: (8, 8), 4: (1, 2), 8: (2, 2)}[blocks]
    split = P("batch", "tm", None)
    return jax.shard_map(
        functools.partial(on_device, ny, nz),
        mesh=mesh,
        in_specs=(split, split, split, P(), P(), P(), P()),
        out_specs=(split, split, split, P(), P(), P(), P()),
        check_vma=False,
    )
```

```python
import functools
import math

import jax
import jax.numpy as jnp
from jax import lax
from jax.experimental import pallas as pl
from jax.experimental.pallas import tpu as pltpu
from jax.sharding import PartitionSpec as P

MESH = pl.DeviceIdType.MESH
F32 = jnp.float32
BF16 = jnp.bfloat16

RES = 64
GATE = 256
SKIP = 128
LAYERS = 5
SEQ = 4
ROWS = 128
N = SEQ * ROWS
DIL = (8, 16, 32, 64, 128)
LOW = (16, 32, 64, 128, 128)
CHUNK = 32
NX = 4
TILES = 8
WIRE = 7


def nn(left, right):
    return jnp.dot(left, right, preferred_element_type=F32)


def nt(left, right):
    return lax.dot_general(left, right, (((1,), (1,)), ((), ())), preferred_element_type=F32)


def tn(left, right):
    return lax.dot_general(left, right, (((0,), (0,)), ((), ())), preferred_element_type=F32)


def far_first(n):
    return sorted(range(1, n), key=lambda r: -min(r, n - r))


def kernel(
    ny, nz, scale,
    signal, skip_grad, stream_grad, w_past, w_now, w_res, w_skip,
    skip_st, stream_st, cot_st, past_st, now_st, res_st, gskip_st,
    sig, sgrad, wres, skipg,
    wx, wb, wf, wg, h2, xs, pre, gated, dfilt, dgate, skip_acc, flow, gcot, flow_b, pcot,
    sig_in, h4_out, h4_in, past_f, past_out, past_in,
    grad, pair_in, half, ring_in, part, part_in, line_in, final,
    load_sem, halo_send, halo_recv, red_send, red_recv,
):
    tm = lax.axis_index("tm")
    batch = lax.axis_index("batch")
    blocks = ny * nz * 2
    x_lo = tm % 2
    core = batch % 2
    xi = (batch // 2) * 2 + x_lo
    zi = (tm // 2) % nz
    yi = tm // (2 * nz)
    ei = core * NX + xi
    tz = TILES // nz

    after = {"tm": (tm + 1) % blocks, "batch": batch}
    before = {"tm": (tm + blocks - 1) % blocks, "batch": batch}
    sibling = {"tm": tm, "batch": batch + 1 - 2 * core}
    x_peers = []
    for r in far_first(NX):
        x = (xi + r) % NX
        x_peers.append((x, {"tm": tm - x_lo + x % 2, "batch": (x // 2) * 2 + core}))
    z_peers = []
    for r in far_first(nz):
        z = (zi + r) % nz
        z_peers.append((z, {"tm": (yi * nz + z) * 2 + x_lo, "batch": batch}))
    y_peers = []
    for r in far_first(ny):
        y = (yi + r) % ny
        y_peers.append((y, {"tm": (y * nz + zi) * 2 + x_lo, "batch": batch}))

    barrier = pltpu.get_barrier_semaphore()
    partners = [before, after, sibling] + [peer for _, peer in x_peers + z_peers + y_peers]
    for partner in partners:
        pl.semaphore_signal(barrier, inc=1, device_id=partner, device_id_type=MESH)

    loads = []

    def load(src, dst):
        copy = pltpu.make_async_copy(src, dst, load_sem.at[len(loads)])
        copy.start()
        loads.append(copy)

    load(signal, sig)
    load(w_res, wres)
    load(w_past, wx.at[:, pl.ds(0, 64), :])
    load(w_now, wx.at[:, pl.ds(64, 64), :])
    load(w_skip, wf.at[:, :, pl.ds(0, 128)])
    load(w_skip, wg.at[:, :, pl.ds(0, 128)])
    load(stream_grad, sgrad)
    load(skip_grad, skipg)
    load(w_past, wb.at[:, pl.ds(0, 64), :])
    load(w_past, wb.at[:, pl.ds(64, 64), :])
    load(w_now, wb.at[:, pl.ds(128, 64), :])
    load(w_now, wb.at[:, pl.ds(192, 64), :])

    pl.semaphore_wait(barrier, len(partners))

    def halo_copy(which, src, dst, target):
        return pltpu.make_async_remote_copy(
            src_ref=src, dst_ref=dst, send_sem=halo_send.at[which], recv_sem=halo_recv.at[which],
            device_id=target, device_id_type=MESH,
        )

    first = halo_copy(5, signal, sig_in, after)
    first.start()

    twice = (
        lax.broadcasted_iota(jnp.int32, (RES, 128), 1) % RES
        == lax.broadcasted_iota(jnp.int32, (RES, 128), 0)
    ).astype(F32).astype(BF16)
    once = (
        lax.broadcasted_iota(jnp.int32, (RES, 128), 1)
        == lax.broadcasted_iota(jnp.int32, (RES, 128), 0)
    ).astype(F32).astype(BF16)
    low_half = lax.broadcasted_iota(jnp.int32, (1, 128), 1) < RES
    has_before = jnp.where(tm > 0, 1.0, 0.0).astype(F32)
    has_after = jnp.where(tm < blocks - 1, 1.0, 0.0).astype(F32)
    skip_acc[...] = jnp.zeros_like(skip_acc)
    loads[0].wait()
    for s in range(SEQ):
        h2[0, s, 128:256, :] = tn(sig[s], twice)
    loads[1].wait()
    for j in range(LAYERS):
        both = tn(wres[j], twice)
        wf[j, :, 128:256] = both.astype(BF16)
        wg[j, :, 128:256] = jnp.where(low_half, both, 0.0).astype(BF16)
    for copy in loads[2:]:
        copy.wait()
    for s in range(SEQ):
        flow[s] = tn(sgrad[s], twice)

    def pack(rows):
        return jnp.where(low_half, rows[0:2], rows[2:4]).astype(BF16)

    def gates(j, lo, hi):
        span = hi - lo
        count = SEQ * span
        d = DIL[j]
        size = CHUNK if span % CHUNK == 0 else 16
        own = max(lo, 128)
        x = jnp.where(low_half, h2[j, :, lo - d : hi - d, :], h2[j, :, lo:hi, :]).astype(BF16)
        xs[j, :, own - 128 : hi - 128, :] = x[:, own - lo :, :]
        pre[0:count, :] = nn(x.reshape(count, 128), wx[j])

        def step(q, carry):
            for c in range(0, span, size):
                rows = pl.ds(pl.multiple_of(q * span + c, 16), size)
                t = jnp.tanh(pre[rows, 0:GATE])
                s = 0.5 * jnp.tanh(0.5 * pre[rows, GATE : 2 * GATE]) + 0.5
                ts = t * s
                gated[j, q, lo + c : lo + c + size, :] = ts.astype(BF16)
                if lo + c + size > 128:
                    dfilt[j, q, lo + c : lo + c + size, :] = s * (1.0 - t * t)
                    dgate[j, q, lo + c : lo + c + size, :] = ts * (1.0 - s)
            return carry

        lax.fori_loop(0, SEQ, step, 0)

    def advance(j, lo, hi):
        span = hi - lo
        count = SEQ * span
        own = max(lo, 128)
        y = nn(gated[j, :, lo:hi, :].reshape(count, GATE), wf[j]).reshape(SEQ, span, 256)
        skip_acc[:, own - 128 : hi - 128, :] += y[:, own - lo :, 0:128]
        new = (h2[j, :, lo:hi, :] + y[:, :, 128:256]).astype(BF16)
        if j + 1 < LAYERS:
            h2[j + 1, :, lo:hi, :] = new.astype(F32)
        return new

    for j in range(3):
        gates(j, LOW[j] + 128, 256)
        advance(j, LOW[j] + 128, 256)
    first.wait()
    for s in range(SEQ):
        h2[0, s, 0:128, :] = has_before * tn(sig_in[s], twice)
    for j in range(3):
        gates(j, LOW[j], LOW[j] + 128)
        advance(j, LOW[j], LOW[j] + 128)
    gates(3, 128, 256)
    new = advance(3, 128, 256)
    h4_out[...] = pack(new.astype(F32))
    second = halo_copy(6, h4_out, h4_in, after)
    second.start()

    def cotangent(j, a, b):
        count = SEQ * (b - a)
        fb = flow[:, a:b, :].astype(BF16)
        flow_b[j, :, a:b, :] = fb
        left = jnp.concatenate([skipg[:, a:b, :], fb], 2).reshape(count, 256)
        gcot[0:count, :] = nt(left, wg[j])

    def back(j, a, b):
        span = b - a
        count = SEQ * span
        size = CHUNK if span % CHUNK == 0 else 16
        per = span // size

        def step(i, carry):
            s = i // per
            here = pl.ds(pl.multiple_of(i * size, 16), size)
            rows = pl.ds(pl.multiple_of(a + (i % per) * size, 16), size)
            held = pl.ds(pl.multiple_of(128 + a + (i % per) * size, 16), size)
            gc = gcot[here, :]
            pcot[j, s, rows, 0:GATE] = (gc * dfilt[j, s, held, :]).astype(BF16)
            pcot[j, s, rows, GATE : 2 * GATE] = (gc * dgate[j, s, held, :]).astype(BF16)
            return carry

        lax.fori_loop(0, SEQ * per, step, 0)
        both = nt(pcot[j, :, a:b, :].reshape(count, 2 * GATE), wb[j])
        past = both[:, 0:128].astype(BF16).reshape(SEQ, span, 128)
        past = past.astype(F32)
        past_f[j, :, a:b, :] = past
        head = min(b, max(DIL[j], 16))
        if a < head:
            past_out[j, :, a:head, :] = pack(past[:, 0 : head - a, :])
        flow[:, a:b, :] += both[:, 128:256].reshape(SEQ, span, 128)

    def head_copy(j):
        rows = pl.ds(0, max(DIL[j], 16))
        return halo_copy(j, past_out.at[j, :, rows, :], past_in.at[j, :, rows, :], before)

    def move(j, a, b):
        d = DIL[j]
        lo, hi = a + d, b + d
        pieces = []
        if lo < ROWS:
            pieces.append(past_f[j, :, lo : min(hi, ROWS), :])
        if hi > ROWS:
            edge = past_in[j, :, 0 : max(d, 16), :].astype(F32)
            turned = pltpu.roll(edge, RES, 2)
            edge = jnp.concatenate(
                [jnp.where(low_half, edge, turned), jnp.where(low_half, turned, edge)], 0
            )
            pieces.append(has_after * edge[:, max(lo - ROWS, 0) : hi - ROWS, :])
        flow[:, a:b, :] += pieces[0] if len(pieces) == 1 else jnp.concatenate(pieces, 1)

    def weight_sums(j):
        gx = tn(xs[j].reshape(N, 128), pcot[j].reshape(N, 2 * GATE))
        right = jnp.concatenate([skipg[...], flow_b[j]], 2).reshape(N, 256)
        gy = tn(gated[j, :, 128:256, :].reshape(N, GATE), right)
        grad[j, :, :, 0:512] = gx.astype(BF16).reshape(2 * NX, 16, 512)
        packed = jnp.where(low_half, gy[0:128, 128:256], gy[128:256, 128:256]).T
        grad[j, :, :, 512:640] = packed.astype(BF16).reshape(2 * NX, 16, 128)
        grad[j, :, :, 640:768] = gy[0:128, 0:128].astype(BF16).reshape(2 * NX, 16, 128)
        grad[j, :, :, 768:896] = gy[128:256, 0:128].astype(BF16).reshape(2 * NX, 16, 128)

    def red_copy(stage, j, src, dst, target):
        pltpu.make_async_remote_copy(
            src_ref=src, dst_ref=dst, send_sem=red_send.at[stage, j], recv_sem=red_recv.at[stage, j],
            device_id=target, device_id_type=MESH,
        ).start()

    def red_wait(sem, ref):
        pltpu.make_async_copy(ref, ref, sem).wait()

    mine = pl.ds(core * NX, NX)
    other = pl.ds((1 - core) * NX, NX)

    def scatter_core(j):
        red_copy(0, j, grad.at[j, other], pair_in.at[j], sibling)

    def scatter_x(j):
        red_wait(red_recv.at[0, j], pair_in.at[j])
        half[j] = (grad[j, mine].astype(F32) + pair_in[j].astype(F32)).astype(BF16)
        for r, (x, peer) in enumerate(x_peers):
            red_copy(1, j, half.at[j, x], ring_in.at[j, r], peer)

    def scatter_z(j):
        red_wait(red_recv.at[1, j], ring_in.at[j])
        total = half[j, xi].astype(F32)
        for r in range(NX - 1):
            total += ring_in[j, r].astype(F32)
        for k in range(WIRE):
            part[j, k // tz, k % tz] = total[:, 128 * k : 128 * k + 128].astype(BF16)
        for k in range(WIRE, TILES):
            part[j, k // tz, k % tz] = jnp.zeros((16, 128), BF16)
        for r, (z, peer) in enumerate(z_peers):
            red_copy(2, j, part.at[j, z], part_in.at[j, r], peer)
        red_wait(red_send.at[0, j], pair_in.at[j])

    def across_y(j):
        if nz > 1:
            red_wait(red_recv.at[2, j], part_in.at[j])
        total = part[j, zi].astype(F32)
        for r in range(nz - 1):
            total += part_in[j, r].astype(F32)
        line_in[j, yi] = total.astype(BF16)
        for _, peer in y_peers:
            red_copy(3, j, line_in.at[j, yi], line_in.at[j, yi], peer)
        red_wait(red_send.at[1, j], ring_in.at[j])

    def gather_z(j):
        if ny > 1:
            red_wait(red_recv.at[3, j], line_in.at[j, pl.ds(0, ny - 1)])
        total = line_in[j, 0].astype(F32)
        for r in range(1, ny):
            total += line_in[j, r].astype(F32)
        final[j, ei, zi] = (total * scale).astype(BF16)
        for _, peer in z_peers:
            red_copy(4, j, final.at[j, ei, zi], final.at[j, ei, zi], peer)
        if nz > 1:
            red_wait(red_send.at[2, j], part_in.at[j])

    def gather_x(j):
        if nz > 1:
            red_wait(red_recv.at[4, j], final.at[j, 0, pl.ds(0, nz - 1)])
        for _, peer in x_peers:
            red_copy(5, j, final.at[j, ei], final.at[j, ei], peer)
        if ny > 1:
            red_wait(red_send.at[3, j], line_in.at[j, pl.ds(0, ny - 1)])

    def gather_core(j):
        red_wait(red_recv.at[5, j], final.at[j, pl.ds(0, NX - 1)])
        red_copy(6, j, final.at[j, mine], final.at[j, mine], sibling)
        if nz > 1:
            red_wait(red_send.at[4, j], final.at[j, 0, pl.ds(0, nz - 1)])
        red_wait(red_send.at[5, j], final.at[j, pl.ds(0, NX - 1)])

    def finish(j):
        red_wait(red_recv.at[6, j], final.at[j, pl.ds(0, NX)])
        tile = [final[j, :, k // tz, k % tz].reshape(128, 128) for k in range(WIRE)]
        for k in range(4):
            past_st[j, :, 128 * k : 128 * k + 128] = tile[k][0:64]
            now_st[j, :, 128 * k : 128 * k + 128] = tile[k][64:128]
        res_st[j, :, 0:128] = tile[4][0:64]
        res_st[j, :, 128:256] = tile[4][64:128]
        gskip_st[j, 0:128, :] = tile[5]
        gskip_st[j, 128:256, :] = tile[6]
        red_wait(red_send.at[6, j], final.at[j, pl.ds(0, NX)])

    stages = (
        scatter_core, scatter_x, scatter_z, across_y, gather_z, gather_x, gather_core, finish
    )

    def turn(*work):
        for k, j in work:
            stages[k](j)

    cotangent(4, 0, ROWS)
    second.wait()
    arrived = has_before * h4_in[...].astype(F32)
    h2[4, 0:2, 0:128, :] = arrived
    h2[4, 2:4, 0:128, :] = pltpu.roll(arrived, RES, 2)
    gates(4, 128, 256)
    heads = [head_copy(j) for j in range(LAYERS)]
    back(4, 0, ROWS)
    heads[4].start()
    new = advance(4, 128, 256)
    for s in range(SEQ):
        stream_st[s] = nt(once, new[s]).astype(BF16)
    skip_st[...] = skip_acc[...].astype(BF16)
    weight_sums(4)
    turn((0, 4))

    heads[4].wait()
    move(4, 0, ROWS)
    cotangent(3, 0, DIL[3])
    back(3, 0, DIL[3])
    heads[3].start()
    cotangent(3, DIL[3], ROWS)
    back(3, DIL[3], ROWS)
    for j in (3, 2, 1):
        d = DIL[j]
        move(j, 0, d)
        cotangent(j - 1, 0, d)
        back(j - 1, 0, d)
        heads[j - 1].start()
    weight_sums(3)
    turn((0, 3), (1, 4))
    during = {
        3: ((0, 2), (1, 3)),
        2: ((0, 1), (1, 2), (2, 4)),
        1: ((0, 0), (1, 1), (1, 0), (2, 3), (2, 2), (3, 4)),
    }
    for j in (3, 2, 1):
        d = DIL[j]
        heads[j].wait()
        move(j, d, ROWS)
        cotangent(j - 1, d, ROWS)
        back(j - 1, d, ROWS)
        weight_sums(j - 1)
        turn(*during[j])
    heads[0].wait()
    move(0, 0, ROWS)
    for s in range(SEQ):
        cot_st[s] = nt(once, flow[s].astype(BF16)).astype(BF16)
    for k in range(2, len(stages)):
        turn((k, 0), (k, 1))
        if k + 1 < len(stages):
            turn((k + 1, 3), (k + 1, 2))
        if k + 2 < len(stages):
            turn((k + 2, 4))


def relay(*refs):
    copies = [pltpu.make_async_copy(refs[i], refs[7 + i], refs[14].at[i]) for i in range(7)]
    for copy in copies:
        copy.start()
    for copy in copies:
        copy.wait()


def on_device(ny, nz, signal, skip_grad, stream_grad, w_past, w_now, w_res, w_skip):
    tz = TILES // nz
    scale = 1.0 / math.sqrt(N * 8 * ny * nz)
    shapes = (
        (SEQ, ROWS, SKIP), (SEQ, RES, ROWS), (SEQ, RES, ROWS),
        (LAYERS, RES, 2 * GATE), (LAYERS, RES, 2 * GATE), (LAYERS, RES, GATE), (LAYERS, GATE, SKIP),
    )
    hbm = pl.BlockSpec(memory_space=pltpu.HBM)
    vmem = pl.BlockSpec(memory_space=pltpu.VMEM)
    bf = functools.partial(pltpu.VMEM, dtype=BF16)
    fp = functools.partial(pltpu.VMEM, dtype=F32)
    outs = pl.pallas_call(
        functools.partial(kernel, ny, nz, scale),
        out_shape=tuple(pltpu.VMEM(s, BF16) for s in shapes),
        in_specs=[hbm] * 7,
        out_specs=(vmem,) * 7,
        scratch_shapes=[
            bf((SEQ, RES, ROWS)),
            bf((SEQ, RES, ROWS)),
            bf((LAYERS, RES, GATE)),
            bf((SEQ, ROWS, SKIP)),
            bf((LAYERS, 128, 512)),
            bf((LAYERS, 256, 512)),
            bf((LAYERS, 256, 256)),
            bf((LAYERS, 256, 256)),
            fp((LAYERS, SEQ, 256, 128)),
            bf((LAYERS, SEQ, ROWS, 128)),
            fp((N, 512)),
            bf((LAYERS, SEQ, 256, 256)),
            fp((LAYERS, SEQ, 256, 256)),
            fp((LAYERS, SEQ, 256, 256)),
            fp((SEQ, ROWS, 128)),
            fp((SEQ, ROWS, 128)),
            fp((N, 256)),
            bf((LAYERS, SEQ, ROWS, 128)),
            bf((LAYERS, SEQ, ROWS, 512)),
            bf((SEQ, RES, ROWS)),
            bf((2, ROWS, 128)),
            bf((2, ROWS, 128)),
            fp((LAYERS, SEQ, ROWS, 128)),
            bf((LAYERS, 2, ROWS, 128)),
            bf((LAYERS, 2, ROWS, 128)),
            bf((LAYERS, 2 * NX, 16, 896)),
            bf((LAYERS, NX, 16, 896)),
            bf((LAYERS, NX, 16, 896)),
            bf((LAYERS, NX - 1, 16, 896)),
            bf((LAYERS, nz, tz, 16, 128)),
            bf((LAYERS, max(nz - 1, 1), tz, 16, 128)),
            bf((LAYERS, ny, tz, 16, 128)),
            bf((LAYERS, 2 * NX, nz, tz, 16, 128)),
            pltpu.SemaphoreType.DMA((12,)),
            pltpu.SemaphoreType.DMA((7,)),
            pltpu.SemaphoreType.DMA((7,)),
            pltpu.SemaphoreType.DMA((7, LAYERS)),
            pltpu.SemaphoreType.DMA((7, LAYERS)),
        ],
        compiler_params=pltpu.CompilerParams(
            collective_id=0, has_side_effects=True, vmem_limit_bytes=44 * 1024 * 1024
        ),
    )(
        *(
            pltpu.with_memory_space_constraint(array, pltpu.HBM)
            for array in (
                jnp.swapaxes(signal, 1, 2), skip_grad, jnp.swapaxes(stream_grad, 1, 2),
                w_past, w_now, jnp.swapaxes(w_res, 1, 2), w_skip,
            )
        )
    )
    outs = pl.pallas_call(
        relay,
        out_shape=tuple(pltpu.HBM(s, BF16) for s in shapes),
        in_specs=[vmem] * 7,
        out_specs=(hbm,) * 7,
        scratch_shapes=[pltpu.SemaphoreType.DMA((7,))],
        compiler_params=pltpu.CompilerParams(vmem_limit_bytes=16 * 1024 * 1024),
    )(*(pltpu.with_memory_space_constraint(array, pltpu.VMEM) for array in outs))
    skip, stream, cot, g_past, g_now, g_res, g_skip = outs
    return (
        skip, jnp.swapaxes(stream, 1, 2), jnp.swapaxes(cot, 1, 2),
        g_past, g_now, jnp.swapaxes(g_res, 1, 2), g_skip,
    )


def solution(mesh):
    blocks = mesh.shape["tm"]
    ny, nz = {128: (8, 8), 4: (1, 2), 8: (2, 2)}[blocks]
    split = P("batch", "tm", None)
    return jax.shard_map(
        functools.partial(on_device, ny, nz),
        mesh=mesh,
        in_specs=(split, split, split, P(), P(), P(), P()),
        out_specs=(split, split, split, P(), P(), P(), P()),
        check_vma=False,
    )
```

```python
import functools
import math

import jax
import jax.numpy as jnp
from jax import lax
from jax.experimental import pallas as pl
from jax.experimental.pallas import tpu as pltpu
from jax.sharding import PartitionSpec as P

MESH = pl.DeviceIdType.MESH
F32 = jnp.float32
BF16 = jnp.bfloat16

RES = 64
GATE = 256
SKIP = 128
LAYERS = 5
SEQ = 4
ROWS = 128
N = SEQ * ROWS
DIL = (8, 16, 32, 64, 128)
LOW = (16, 32, 64, 128, 128)
CHUNK = 32
NX = 4
TILES = 8
WIRE = 7


def nn(left, right):
    return jnp.dot(left, right, preferred_element_type=F32)


def nt(left, right):
    return lax.dot_general(left, right, (((1,), (1,)), ((), ())), preferred_element_type=F32)


def tn(left, right):
    return lax.dot_general(left, right, (((0,), (0,)), ((), ())), preferred_element_type=F32)


def far_first(n):
    return sorted(range(1, n), key=lambda r: -min(r, n - r))


def kernel(
    ny, nz, scale,
    signal, skip_grad, stream_grad, w_past, w_now, w_res, w_skip,
    skip_st, stream_st, cot_st, past_st, now_st, res_st, gskip_st,
    sig, sgrad, wres, skipg,
    wx, wb, wf, wg, h2, xs, pre, gated, dfilt, dgate, skip_acc, flow, gcot, flow_b, pcot,
    sig_in, h4_out, h4_in, past_f, past_out, past_in,
    grad, pair_in, half, ring_in, part, part_in, line_in, final,
    load_sem, halo_send, halo_recv, red_send, red_recv,
):
    tm = lax.axis_index("tm")
    batch = lax.axis_index("batch")
    blocks = ny * nz * 2
    x_lo = tm % 2
    core = batch % 2
    xi = (batch // 2) * 2 + x_lo
    zi = (tm // 2) % nz
    yi = tm // (2 * nz)
    ei = core * NX + xi
    tz = TILES // nz
    filled = pl.ds(0, -(-WIRE // tz))

    after = {"tm": (tm + 1) % blocks, "batch": batch}
    before = {"tm": (tm + blocks - 1) % blocks, "batch": batch}
    sibling = {"tm": tm, "batch": batch + 1 - 2 * core}
    x_peers = []
    for r in far_first(NX):
        x = (xi + r) % NX
        x_peers.append((x, {"tm": tm - x_lo + x % 2, "batch": (x // 2) * 2 + core}))
    z_peers = []
    for r in far_first(nz):
        z = (zi + r) % nz
        z_peers.append((z, {"tm": (yi * nz + z) * 2 + x_lo, "batch": batch}))
    y_peers = []
    for r in far_first(ny):
        y = (yi + r) % ny
        y_peers.append((y, {"tm": (y * nz + zi) * 2 + x_lo, "batch": batch}))

    barrier = pltpu.get_barrier_semaphore()
    partners = [before, after, sibling] + [peer for _, peer in x_peers + z_peers + y_peers]
    for partner in partners:
        pl.semaphore_signal(barrier, inc=1, device_id=partner, device_id_type=MESH)

    loads = []

    def load(src, dst):
        copy = pltpu.make_async_copy(src, dst, load_sem.at[len(loads)])
        copy.start()
        loads.append(copy)

    load(signal, sig)
    load(w_res, wres)
    load(w_past, wx.at[:, pl.ds(0, 64), :])
    load(w_now, wx.at[:, pl.ds(64, 64), :])
    load(w_skip, wf.at[:, :, pl.ds(0, 128)])
    load(w_skip, wg.at[:, :, pl.ds(0, 128)])
    load(stream_grad, sgrad)
    load(skip_grad, skipg)
    load(w_past, wb.at[:, pl.ds(0, 64), :])
    load(w_past, wb.at[:, pl.ds(64, 64), :])
    load(w_now, wb.at[:, pl.ds(128, 64), :])
    load(w_now, wb.at[:, pl.ds(192, 64), :])

    pl.semaphore_wait(barrier, len(partners))

    def halo_copy(which, src, dst, target):
        return pltpu.make_async_remote_copy(
            src_ref=src, dst_ref=dst, send_sem=halo_send.at[which], recv_sem=halo_recv.at[which],
            device_id=target, device_id_type=MESH,
        )

    first = halo_copy(5, signal, sig_in, after)
    first.start()

    twice = (
        lax.broadcasted_iota(jnp.int32, (RES, 128), 1) % RES
        == lax.broadcasted_iota(jnp.int32, (RES, 128), 0)
    ).astype(F32).astype(BF16)
    once = (
        lax.broadcasted_iota(jnp.int32, (RES, 128), 1)
        == lax.broadcasted_iota(jnp.int32, (RES, 128), 0)
    ).astype(F32).astype(BF16)
    low_half = lax.broadcasted_iota(jnp.int32, (1, 128), 1) < RES
    has_before = jnp.where(tm > 0, 1.0, 0.0).astype(F32)
    has_after = jnp.where(tm < blocks - 1, 1.0, 0.0).astype(F32)
    skip_acc[...] = jnp.zeros_like(skip_acc)
    loads[0].wait()
    for s in range(SEQ):
        h2[0, s, 128:256, :] = tn(sig[s], twice)
    loads[1].wait()
    for j in range(LAYERS):
        both = tn(wres[j], twice)
        wf[j, :, 128:256] = both.astype(BF16)
        wg[j, :, 128:256] = jnp.where(low_half, both, 0.0).astype(BF16)
    for copy in loads[2:]:
        copy.wait()
    for s in range(SEQ):
        flow[s] = tn(sgrad[s], twice)

    def pack(rows):
        return jnp.where(low_half, rows[0:2], rows[2:4]).astype(BF16)

    def gates(j, lo, hi):
        span = hi - lo
        count = SEQ * span
        d = DIL[j]
        size = CHUNK if span % CHUNK == 0 else 16
        own = max(lo, 128)
        x = jnp.where(low_half, h2[j, :, lo - d : hi - d, :], h2[j, :, lo:hi, :]).astype(BF16)
        xs[j, :, own - 128 : hi - 128, :] = x[:, own - lo :, :]
        pre[0:count, :] = nn(x.reshape(count, 128), wx[j])

        def step(q, carry):
            for c in range(0, span, size):
                rows = pl.ds(pl.multiple_of(q * span + c, 16), size)
                t = jnp.tanh(pre[rows, 0:GATE])
                s = 0.5 * jnp.tanh(0.5 * pre[rows, GATE : 2 * GATE]) + 0.5
                ts = t * s
                gated[j, q, lo + c : lo + c + size, :] = ts.astype(BF16)
                if lo + c + size > 128:
                    dfilt[j, q, lo + c : lo + c + size, :] = s * (1.0 - t * t)
                    dgate[j, q, lo + c : lo + c + size, :] = ts * (1.0 - s)
            return carry

        lax.fori_loop(0, SEQ, step, 0)

    def advance(j, lo, hi):
        span = hi - lo
        count = SEQ * span
        own = max(lo, 128)
        y = nn(gated[j, :, lo:hi, :].reshape(count, GATE), wf[j]).reshape(SEQ, span, 256)
        skip_acc[:, own - 128 : hi - 128, :] += y[:, own - lo :, 0:128]
        new = (h2[j, :, lo:hi, :] + y[:, :, 128:256]).astype(BF16)
        if j + 1 < LAYERS:
            h2[j + 1, :, lo:hi, :] = new.astype(F32)
        return new

    for j in range(3):
        gates(j, LOW[j] + 128, 256)
        advance(j, LOW[j] + 128, 256)
    first.wait()
    for s in range(SEQ):
        h2[0, s, 0:128, :] = has_before * tn(sig_in[s], twice)
    for j in range(3):
        gates(j, LOW[j], LOW[j] + 128)
        advance(j, LOW[j], LOW[j] + 128)
    gates(3, 128, 256)
    new = advance(3, 128, 256)
    h4_out[...] = pack(new.astype(F32))
    second = halo_copy(6, h4_out, h4_in, after)
    second.start()

    def cotangent(j, a, b):
        count = SEQ * (b - a)
        fb = flow[:, a:b, :].astype(BF16)
        flow_b[j, :, a:b, :] = fb
        left = jnp.concatenate([skipg[:, a:b, :], fb], 2).reshape(count, 256)
        gcot[0:count, :] = nt(left, wg[j])

    def back(j, a, b):
        span = b - a
        count = SEQ * span
        size = CHUNK if span % CHUNK == 0 else 16
        per = span // size

        def step(i, carry):
            s = i // per
            here = pl.ds(pl.multiple_of(i * size, 16), size)
            rows = pl.ds(pl.multiple_of(a + (i % per) * size, 16), size)
            held = pl.ds(pl.multiple_of(128 + a + (i % per) * size, 16), size)
            gc = gcot[here, :]
            pcot[j, s, rows, 0:GATE] = (gc * dfilt[j, s, held, :]).astype(BF16)
            pcot[j, s, rows, GATE : 2 * GATE] = (gc * dgate[j, s, held, :]).astype(BF16)
            return carry

        lax.fori_loop(0, SEQ * per, step, 0)
        both = nt(pcot[j, :, a:b, :].reshape(count, 2 * GATE), wb[j])
        past = both[:, 0:128].astype(BF16).reshape(SEQ, span, 128)
        past = past.astype(F32)
        past_f[j, :, a:b, :] = past
        head = min(b, max(DIL[j], 16))
        if a < head:
            past_out[j, :, a:head, :] = pack(past[:, 0 : head - a, :])
        flow[:, a:b, :] += both[:, 128:256].reshape(SEQ, span, 128)

    def head_copy(j):
        rows = pl.ds(0, max(DIL[j], 16))
        return halo_copy(j, past_out.at[j, :, rows, :], past_in.at[j, :, rows, :], before)

    def move(j, a, b):
        d = DIL[j]
        lo, hi = a + d, b + d
        pieces = []
        if lo < ROWS:
            pieces.append(past_f[j, :, lo : min(hi, ROWS), :])
        if hi > ROWS:
            edge = past_in[j, :, 0 : max(d, 16), :].astype(F32)
            turned = pltpu.roll(edge, RES, 2)
            edge = jnp.concatenate(
                [jnp.where(low_half, edge, turned), jnp.where(low_half, turned, edge)], 0
            )
            pieces.append(has_after * edge[:, max(lo - ROWS, 0) : hi - ROWS, :])
        flow[:, a:b, :] += pieces[0] if len(pieces) == 1 else jnp.concatenate(pieces, 1)

    def weight_sums(j):
        gx = tn(xs[j].reshape(N, 128), pcot[j].reshape(N, 2 * GATE))
        right = jnp.concatenate([skipg[...], flow_b[j]], 2).reshape(N, 256)
        gy = tn(gated[j, :, 128:256, :].reshape(N, GATE), right)
        grad[j, :, :, 0:512] = gx.astype(BF16).reshape(2 * NX, 16, 512)
        packed = jnp.where(low_half, gy[0:128, 128:256], gy[128:256, 128:256]).T
        grad[j, :, :, 512:640] = packed.astype(BF16).reshape(2 * NX, 16, 128)
        grad[j, :, :, 640:768] = gy[0:128, 0:128].astype(BF16).reshape(2 * NX, 16, 128)
        grad[j, :, :, 768:896] = gy[128:256, 0:128].astype(BF16).reshape(2 * NX, 16, 128)

    def red_copy(stage, j, src, dst, target):
        pltpu.make_async_remote_copy(
            src_ref=src, dst_ref=dst, send_sem=red_send.at[stage, j], recv_sem=red_recv.at[stage, j],
            device_id=target, device_id_type=MESH,
        ).start()

    def red_wait(sem, ref):
        pltpu.make_async_copy(ref, ref, sem).wait()

    mine = pl.ds(core * NX, NX)
    other = pl.ds((1 - core) * NX, NX)

    def scatter_core(j):
        red_copy(0, j, grad.at[j, other], pair_in.at[j], sibling)

    def scatter_x(j):
        red_wait(red_recv.at[0, j], pair_in.at[j])
        half[j] = (grad[j, mine].astype(F32) + pair_in[j].astype(F32)).astype(BF16)
        for r, (x, peer) in enumerate(x_peers):
            red_copy(1, j, half.at[j, x], ring_in.at[j, r], peer)

    def scatter_z(j):
        red_wait(red_recv.at[1, j], ring_in.at[j])
        total = half[j, xi].astype(F32)
        for r in range(NX - 1):
            total += ring_in[j, r].astype(F32)
        for k in range(WIRE):
            part[j, k // tz, k % tz] = total[:, 128 * k : 128 * k + 128].astype(BF16)
        for k in range(WIRE, TILES):
            part[j, k // tz, k % tz] = jnp.zeros((16, 128), BF16)
        for r, (z, peer) in enumerate(z_peers):
            red_copy(2, j, part.at[j, z], part_in.at[j, r], peer)
        red_wait(red_send.at[0, j], pair_in.at[j])

    def across_y(j):
        if nz > 1:
            red_wait(red_recv.at[2, j], part_in.at[j])
        total = part[j, zi].astype(F32)
        for r in range(nz - 1):
            total += part_in[j, r].astype(F32)
        line_in[j, yi] = total.astype(BF16)
        for _, peer in y_peers:
            red_copy(3, j, line_in.at[j, yi], line_in.at[j, yi], peer)
        red_wait(red_send.at[1, j], ring_in.at[j])

    def gather_z(j):
        if ny > 1:
            red_wait(red_recv.at[3, j], line_in.at[j, pl.ds(0, ny - 1)])
        total = line_in[j, 0].astype(F32)
        for r in range(1, ny):
            total += line_in[j, r].astype(F32)
        final[j, ei, zi] = (total * scale).astype(BF16)
        for _, peer in z_peers:
            red_copy(4, j, final.at[j, ei, zi], final.at[j, ei, zi], peer)
        if nz > 1:
            red_wait(red_send.at[2, j], part_in.at[j])

    def gather_x(j):
        if nz > 1:
            red_wait(red_recv.at[4, j], final.at[j, 0, pl.ds(0, nz - 1)])
        for _, peer in x_peers:
            red_copy(5, j, final.at[j, ei, filled], final.at[j, ei, filled], peer)
        if ny > 1:
            red_wait(red_send.at[3, j], line_in.at[j, pl.ds(0, ny - 1)])

    def gather_core(j):
        red_wait(red_recv.at[5, j], final.at[j, pl.ds(0, NX - 1), filled])
        red_copy(6, j, final.at[j, mine, filled], final.at[j, mine, filled], sibling)
        if nz > 1:
            red_wait(red_send.at[4, j], final.at[j, 0, pl.ds(0, nz - 1)])
        red_wait(red_send.at[5, j], final.at[j, pl.ds(0, NX - 1), filled])

    def finish(j):
        red_wait(red_recv.at[6, j], final.at[j, pl.ds(0, NX), filled])
        tile = [final[j, :, k // tz, k % tz].reshape(128, 128) for k in range(WIRE)]
        for k in range(4):
            past_st[j, :, 128 * k : 128 * k + 128] = tile[k][0:64]
            now_st[j, :, 128 * k : 128 * k + 128] = tile[k][64:128]
        res_st[j, :, 0:128] = tile[4][0:64]
        res_st[j, :, 128:256] = tile[4][64:128]
        gskip_st[j, 0:128, :] = tile[5]
        gskip_st[j, 128:256, :] = tile[6]
        red_wait(red_send.at[6, j], final.at[j, pl.ds(0, NX), filled])

    stages = (
        scatter_core, scatter_x, scatter_z, across_y, gather_z, gather_x, gather_core, finish
    )

    def turn(*work):
        for k, j in work:
            stages[k](j)

    cotangent(4, 0, ROWS)
    second.wait()
    arrived = has_before * h4_in[...].astype(F32)
    h2[4, 0:2, 0:128, :] = arrived
    h2[4, 2:4, 0:128, :] = pltpu.roll(arrived, RES, 2)
    gates(4, 128, 256)
    heads = [head_copy(j) for j in range(LAYERS)]
    back(4, 0, ROWS)
    heads[4].start()
    new = advance(4, 128, 256)
    for s in range(SEQ):
        stream_st[s] = nt(once, new[s]).astype(BF16)
    skip_st[...] = skip_acc[...].astype(BF16)
    weight_sums(4)
    turn((0, 4))

    heads[4].wait()
    move(4, 0, ROWS)
    cotangent(3, 0, DIL[3])
    back(3, 0, DIL[3])
    heads[3].start()
    cotangent(3, DIL[3], ROWS)
    back(3, DIL[3], ROWS)
    for j in (3, 2, 1):
        d = DIL[j]
        move(j, 0, d)
        cotangent(j - 1, 0, d)
        back(j - 1, 0, d)
        heads[j - 1].start()
    weight_sums(3)
    turn((0, 3), (1, 4))
    during = {
        3: ((0, 2), (1, 3)),
        2: ((0, 1), (1, 2), (2, 4)),
        1: ((0, 0), (1, 1), (1, 0), (2, 3), (2, 2), (3, 4)),
    }
    for j in (3, 2, 1):
        d = DIL[j]
        heads[j].wait()
        move(j, d, ROWS)
        cotangent(j - 1, d, ROWS)
        back(j - 1, d, ROWS)
        weight_sums(j - 1)
        turn(*during[j])
    heads[0].wait()
    move(0, 0, ROWS)
    for s in range(SEQ):
        cot_st[s] = nt(once, flow[s].astype(BF16)).astype(BF16)
    for k in range(2, len(stages)):
        turn((k, 0), (k, 1))
        if k + 1 < len(stages):
            turn((k + 1, 3), (k + 1, 2))
        if k + 2 < len(stages):
            turn((k + 2, 4))


def relay(*refs):
    copies = [pltpu.make_async_copy(refs[i], refs[7 + i], refs[14].at[i]) for i in range(7)]
    for copy in copies:
        copy.start()
    for copy in copies:
        copy.wait()


def on_device(ny, nz, signal, skip_grad, stream_grad, w_past, w_now, w_res, w_skip):
    tz = TILES // nz
    scale = 1.0 / math.sqrt(N * 8 * ny * nz)
    shapes = (
        (SEQ, ROWS, SKIP), (SEQ, RES, ROWS), (SEQ, RES, ROWS),
        (LAYERS, RES, 2 * GATE), (LAYERS, RES, 2 * GATE), (LAYERS, RES, GATE), (LAYERS, GATE, SKIP),
    )
    hbm = pl.BlockSpec(memory_space=pltpu.HBM)
    vmem = pl.BlockSpec(memory_space=pltpu.VMEM)
    bf = functools.partial(pltpu.VMEM, dtype=BF16)
    fp = functools.partial(pltpu.VMEM, dtype=F32)
    outs = pl.pallas_call(
        functools.partial(kernel, ny, nz, scale),
        out_shape=tuple(pltpu.VMEM(s, BF16) for s in shapes),
        in_specs=[hbm] * 7,
        out_specs=(vmem,) * 7,
        scratch_shapes=[
            bf((SEQ, RES, ROWS)),
            bf((SEQ, RES, ROWS)),
            bf((LAYERS, RES, GATE)),
            bf((SEQ, ROWS, SKIP)),
            bf((LAYERS, 128, 512)),
            bf((LAYERS, 256, 512)),
            bf((LAYERS, 256, 256)),
            bf((LAYERS, 256, 256)),
            fp((LAYERS, SEQ, 256, 128)),
            bf((LAYERS, SEQ, ROWS, 128)),
            fp((N, 512)),
            bf((LAYERS, SEQ, 256, 256)),
            fp((LAYERS, SEQ, 256, 256)),
            fp((LAYERS, SEQ, 256, 256)),
            fp((SEQ, ROWS, 128)),
            fp((SEQ, ROWS, 128)),
            fp((N, 256)),
            bf((LAYERS, SEQ, ROWS, 128)),
            bf((LAYERS, SEQ, ROWS, 512)),
            bf((SEQ, RES, ROWS)),
            bf((2, ROWS, 128)),
            bf((2, ROWS, 128)),
            fp((LAYERS, SEQ, ROWS, 128)),
            bf((LAYERS, 2, ROWS, 128)),
            bf((LAYERS, 2, ROWS, 128)),
            bf((LAYERS, 2 * NX, 16, 896)),
            bf((LAYERS, NX, 16, 896)),
            bf((LAYERS, NX, 16, 896)),
            bf((LAYERS, NX - 1, 16, 896)),
            bf((LAYERS, nz, tz, 16, 128)),
            bf((LAYERS, max(nz - 1, 1), tz, 16, 128)),
            bf((LAYERS, ny, tz, 16, 128)),
            bf((LAYERS, 2 * NX, nz, tz, 16, 128)),
            pltpu.SemaphoreType.DMA((12,)),
            pltpu.SemaphoreType.DMA((7,)),
            pltpu.SemaphoreType.DMA((7,)),
            pltpu.SemaphoreType.DMA((7, LAYERS)),
            pltpu.SemaphoreType.DMA((7, LAYERS)),
        ],
        compiler_params=pltpu.CompilerParams(
            collective_id=0, has_side_effects=True, vmem_limit_bytes=44 * 1024 * 1024
        ),
    )(
        *(
            pltpu.with_memory_space_constraint(array, pltpu.HBM)
            for array in (
                jnp.swapaxes(signal, 1, 2), skip_grad, jnp.swapaxes(stream_grad, 1, 2),
                w_past, w_now, jnp.swapaxes(w_res, 1, 2), w_skip,
            )
        )
    )
    outs = pl.pallas_call(
        relay,
        out_shape=tuple(pltpu.HBM(s, BF16) for s in shapes),
        in_specs=[vmem] * 7,
        out_specs=(hbm,) * 7,
        scratch_shapes=[pltpu.SemaphoreType.DMA((7,))],
        compiler_params=pltpu.CompilerParams(vmem_limit_bytes=16 * 1024 * 1024),
    )(*(pltpu.with_memory_space_constraint(array, pltpu.VMEM) for array in outs))
    skip, stream, cot, g_past, g_now, g_res, g_skip = outs
    return (
        skip, jnp.swapaxes(stream, 1, 2), jnp.swapaxes(cot, 1, 2),
        g_past, g_now, jnp.swapaxes(g_res, 1, 2), g_skip,
    )


def solution(mesh):
    blocks = mesh.shape["tm"]
    ny, nz = {128: (8, 8), 4: (1, 2), 8: (2, 2)}[blocks]
    split = P("batch", "tm", None)
    return jax.shard_map(
        functools.partial(on_device, ny, nz),
        mesh=mesh,
        in_specs=(split, split, split, P(), P(), P(), P()),
        out_specs=(split, split, split, P(), P(), P(), P()),
        check_vma=False,
    )
```
